128 devices in a mesh: state: 16 (over y, x_hi, core), walk: 8 (over z, x_lo).
Axes of the slice: x: 4 (x_hi: 2, x_lo: 2; x = x_hi * 2 + x_lo), y: 4, z: 4, core: 2. Of those that a mesh axis runs over, the one named last changes fastest.
Arguments:
- features: bfloat16 [16, 8, 512, 256], P('state', 'walk'), may hold values from -6 to 6
- key_blocks: int32 [16, 8, 4, 3], P('state', 'walk'), may hold values from 0 to 3, as said below
- block_counts: int32 [16, 8, 4], P('state', 'walk'), may hold values from 1 to 3, as said below
- potential: float32 [16, 8], P('state', 'walk'), may hold values from -14 to -0.7
- w_qkv: bfloat16 [16, 2, 256, 768], P('state'), may hold values from -1 to 1
- w_out: bfloat16 [16, 2, 256, 256], P('state'), may hold values from -0.375 to 0.375
- w_up: bfloat16 [16, 2, 256, 512], P('state'), may hold values from -0.375 to 0.375
- w_down: bfloat16 [16, 2, 512, 256], P('state'), may hold values from -0.25 to 0.25
- gains: float32 [16, 5, 256], P('state'), may hold values from 0.25 to 1.75
- readouts: float32 [16, 2, 256], P('state'), may hold values from -0.375 to 0.375
Outputs:
- energies: float32 [16, 16, 8], P('state', None, 'walk')
- mean_energy: float32 [16, 16], P('state')
The draws below stay inside these ranges and needn't reach their ends.
Inputs may be any that keep to these rules, and one draw needn't show every extreme that they name: `key_blocks`: slot 0 of block b's list is b itself; the entries of a list are distinct blocks; entries at slots at or past the count are ignored. `block_counts`: block 0 of every configuration has a full list of 3 blocks.
All inputs are finite; a program needn't handle non-finite values.
Results may differ from the reference program's by a relative error of at most 0.04.
Values may be sent and summed in bfloat16 or wider, within the bound.
A program may use at most 128 MiB of HBM per device.

```python
import math
import jax
import jax.numpy as jnp
from jax import lax

D = 256
FF = 512
HEADS = 8
LAYERS = 2
ATOMS = 512
BLOCK = 128
MAXNB = 3
WALKERS = 8
STATES = 16


def draw_features(key, part):
    full_shape = (STATES, WALKERS, ATOMS, D)
    entries = jnp.clip(jax.random.normal(jax.random.fold_in(key, 31), full_shape, jnp.float32), -6.0, 6.0)
    return entries.astype(jnp.bfloat16)


def draw_w_qkv(key, part):
    full_shape = (STATES, LAYERS, D, 3 * D)
    entries = jnp.clip(jax.random.normal(jax.random.fold_in(key, 67), full_shape, jnp.float32), -4.0, 4.0) / math.sqrt(D)
    return entries.astype(jnp.bfloat16)


def draw_potential(key, part):
    magnitude = jnp.exp(jax.random.uniform(jax.random.fold_in(key, 73), (STATES, WALKERS), jnp.float32, math.log(0.7), math.log(14.0)))
    return (-magnitude).astype(jnp.float32)


def draw_key_blocks(key, part):
    nblocks = ATOMS // BLOCK
    total = STATES * WALKERS * nblocks
    subkey = jax.random.fold_in(key, 11)
    row_keys = jax.random.split(subkey, total)
    others = jax.vmap(lambda k: jax.random.permutation(k, nblocks - 1) + 1)(row_keys)
    own = jnp.arange(total, dtype=jnp.int32) % nblocks
    offsets = jnp.concatenate([jnp.zeros((total, 1), jnp.int32), others[:, :MAXNB - 1].astype(jnp.int32)], axis=1)
    lists = (own[:, None] + offsets) % nblocks
    return lists.reshape(STATES, WALKERS, nblocks, MAXNB).astype(jnp.int32)


def draw_block_counts(key, part):
    nblocks = ATOMS // BLOCK
    subkey = jax.random.fold_in(key, 23)
    counts = jax.random.randint(subkey, (STATES, WALKERS, nblocks), 1, MAXNB + 1)
    counts = counts.at[:, :, 0].set(MAXNB)
    return counts.astype(jnp.int32)


def steps_of(key, shape, cuts, smallest, top_value):
    level, own = 1.0, jax.random.fold_in(key, 6)
    for axis_at, parts in cuts:
        heights = jnp.exp(jax.random.uniform(jax.random.fold_in(own, axis_at), (parts,), jnp.float32, smallest / len(cuts), top_value / len(cuts)))
        level = level * jnp.repeat(heights, shape[axis_at] // parts).reshape([-1 if axis == axis_at else 1 for axis in range(len(shape))])
    return level


def centred(key, shape, scale, bound, pieces=(), kind=jnp.bfloat16):
    values = scale * jax.random.normal(key, shape, jnp.float32)
    if pieces:
        values = values * steps_of(key, shape, pieces, -0.22, 0.18)
    return jnp.clip(values, -bound, bound).astype(kind)


def setup_inputs(seed: int = 0) -> dict:
    streams_of = jax.random.split(jax.random.key(seed), 11)
    features = draw_features(jax.random.fold_in(streams_of[10], 71), 0)
    key_blocks = draw_key_blocks(jax.random.fold_in(streams_of[10], 71), 0)
    block_counts = draw_block_counts(jax.random.fold_in(streams_of[10], 71), 0)
    potential = draw_potential(jax.random.fold_in(streams_of[10], 71), 0)
    w_qkv = draw_w_qkv(jax.random.fold_in(streams_of[10], 71), 0)
    w_out = centred(streams_of[5], (STATES, LAYERS, D, D), D ** -0.5, 0.375, ((0, 16),))
    w_up = centred(streams_of[6], (STATES, LAYERS, D, FF), D ** -0.5, 0.375, ((0, 16),))
    w_down = centred(streams_of[7], (STATES, LAYERS, FF, D), FF ** -0.5, 0.25, ((0, 16),))
    gains = jnp.clip(1.0 + 0.15 * jax.random.normal(streams_of[8], (STATES, 2 * LAYERS + 1, D), jnp.float32), 0.25, 1.75)
    readouts = centred(streams_of[9], (STATES, 2, D), D ** -0.5, 0.375, ((0, 16),), jnp.float32)
    return {"features": features, "key_blocks": key_blocks, "block_counts": block_counts, "potential": potential, "w_qkv": w_qkv, "w_out": w_out, "w_up": w_up, "w_down": w_down, "gains": gains, "readouts": readouts}


def rms_norm(value, gain):
    return value * lax.rsqrt(lax.optimization_barrier(jnp.mean(value * value, axis=-1, keepdims=True)) + 1e-06) * gain

def evaluate(w_qkv, w_out, w_up, w_down, gains, readouts, feats, lists, counts):
    atoms, width = feats.shape
    nblocks = atoms // BLOCK
    slots = lists.shape[-1]
    head_dim = width // HEADS
    hidden = feats.astype(jnp.float32)
    valid = jnp.arange(slots)[None, :] < counts[:, None]
    keymask = jnp.repeat(valid, BLOCK, axis=1)
    layers = w_qkv.shape[0]
    for layer in range(layers):
        normed = rms_norm(hidden, gains[2 * layer]).astype(jnp.bfloat16)
        proj = jnp.dot(normed.astype(jnp.float32), w_qkv[layer].astype(jnp.float32), preferred_element_type=jnp.float32).astype(jnp.bfloat16)
        query = proj[:, :width].reshape(nblocks, BLOCK, HEADS, head_dim)
        keyval = proj[:, width:].reshape(nblocks, BLOCK, 2 * width)
        picked = keyval[lists].reshape(nblocks, slots * BLOCK, 2 * width)
        keys = picked[:, :, :width].reshape(nblocks, slots * BLOCK, HEADS, head_dim)
        values = picked[:, :, width:].reshape(nblocks, slots * BLOCK, HEADS, head_dim)
        scores = jnp.einsum('qahd,qkhd->qhak', query.astype(jnp.float32), keys.astype(jnp.float32)) / jnp.sqrt(jnp.float32(head_dim))
        scores = jnp.where(keymask[:, None, None, :], scores, jnp.float32(-1e+30))
        top = lax.optimization_barrier(jnp.max(scores, axis=-1, keepdims=True))
        expo = jnp.exp(scores - top)
        probs = (expo / lax.optimization_barrier(jnp.sum(expo, axis=-1, keepdims=True))).astype(jnp.bfloat16)
        attended = jnp.einsum('qhak,qkhd->qahd', probs.astype(jnp.float32), values.astype(jnp.float32))
        attended = attended.astype(jnp.bfloat16).reshape(atoms, width)
        hidden = hidden + jnp.dot(attended.astype(jnp.float32), w_out[layer].astype(jnp.float32), preferred_element_type=jnp.float32)
        normed = rms_norm(hidden, gains[2 * layer + 1]).astype(jnp.bfloat16)
        upper = jax.nn.gelu(jnp.dot(normed.astype(jnp.float32), w_up[layer].astype(jnp.float32), preferred_element_type=jnp.float32)).astype(jnp.bfloat16)
        hidden = hidden + jnp.dot(upper.astype(jnp.float32), w_down[layer].astype(jnp.float32), preferred_element_type=jnp.float32)
    final = rms_norm(hidden, gains[2 * layers])
    pooled = lax.optimization_barrier(jnp.sum(final, axis=0)) / jnp.sqrt(jnp.float32(atoms))
    return (jnp.sum(pooled * readouts[0]), jnp.sum(pooled * readouts[1]))

def reference(features, key_blocks, block_counts, potential, w_qkv, w_out, w_up, w_down, gains, readouts):

    def one_state(i):

        def one_config(flat):
            j = flat // WALKERS
            w = flat % WALKERS
            return evaluate(w_qkv[i], w_out[i], w_up[i], w_down[i], gains[i], readouts[i], features[j, w], key_blocks[j, w], block_counts[j, w])
        amp, ham = lax.map(one_config, jnp.arange(STATES * WALKERS, dtype=jnp.int32))
        return (amp.reshape(STATES, WALKERS), ham.reshape(STATES, WALKERS))
    amp_raw, ham = lax.map(one_state, jnp.arange(STATES, dtype=jnp.int32))
    ident = jnp.eye(STATES, dtype=jnp.float32)[:, :, None]
    psi = ident + 0.9 / STATES * jnp.tanh(amp_raw)
    solved = jnp.linalg.solve(jnp.transpose(psi, (2, 0, 1)), jnp.transpose(ham, (2, 0, 1)))
    energies = jnp.transpose(solved, (1, 2, 0)) + ident * potential[:, None, :]
    mean_energy = lax.optimization_barrier(jnp.sum(energies, axis=-1)) / WALKERS
    return (energies, mean_energy)
```

```python
import functools

import jax
import jax.numpy as jnp
from jax import lax
from jax.experimental import pallas as pl
from jax.experimental.pallas import tpu as pltpu
from jax.sharding import PartitionSpec as P

D = 256
A = 512
B = 128
NB = 4
H = 8
EXTRA = 16
GROUPS = (1, 3, 4, 8)
QS = 1.4426950408889634 / 32.0**0.5
bf = jnp.bfloat16
f32 = jnp.float32
MESH = pl.DeviceIdType.MESH


def mm(a, b):
    return lax.dot_general(a, b, (((1,), (0,)), ((), ())), preferred_element_type=f32)

def rscale(h):
    return lax.rsqrt(jnp.sum(h*h,axis=0,keepdims=True)*(1.0/D)+1e-6)
def norm(h,g):
    r=rscale(h)
    return jnp.concatenate([((h[:,c:c+128]*r[:,c:c+128])*g).astype(bf) for c in range(0,h.shape[1],128)],axis=1)

def kernel(n,*refs):
    xs=refs[:n]
    wqkv,wo,wu,wd,gn,gr,out=refs[n:n+7]
    xbuf,h_ref,k_ref,v_ref,qx_ref,a_ref,lim,ivm,ism,xsem,isem=refs[n+7:]
    qx_ref[...]=jnp.zeros(qx_ref.shape,bf)
    v_ref[...]=jnp.ones(v_ref.shape,bf)
    def fetch(i):
        for j in range(n):
            @pl.when(i==j)
            def _():
                pltpu.make_async_copy(xs[j],xbuf.at[j%2],xsem.at[j%2]).start()
    def fetched(i):
        s=lax.rem(i,2)
        pltpu.make_async_copy(xs[0],xbuf.at[s],xsem.at[s]).wait()
    def ints(i):
        s=lax.rem(i,2)
        ivm[...]=xbuf[s,D:D+EXTRA,0:128].astype(f32).astype(jnp.int32)
        return pltpu.make_async_copy(ivm,ism.at[s],isem)

    def qkv(l,c,h):
        nc=norm(h,gn[2*l])
        q=(mm(wqkv[l,0:256,:],nc)*QS).astype(bf)
        kk=mm(wqkv[l,256:512,:],nc).astype(bf).T
        v=mm(wqkv[l,512:768,:],nc).astype(bf)
        for hh in range(H):
            p=hh//2; row=(hh%4)*32; lane=(hh%2)*128
            for bb in range(2):
                qx_ref[2*c+bb,p,row:row+32,lane:lane+128]=q[hh*32:hh*32+32,bb*128:bb*128+128]
        for bb in range(2):
            k_ref[2*c+bb]=kk[bb*128:bb*128+128,:]
            for p in range(4):
                v_ref[2*c+bb,p,0:64,:]=v[p*64:p*64+64,bb*128:bb*128+128]

    def attention(slot,safe):
        def run(items):
            units=[(b,kbs,p) for p in range(4) for b,kbs in items]
            def scores(b,kbs,p):
                half=p//2
                return [mm(k_ref[kb,:,half*128:half*128+128],qx_ref[b,p]) for kb in kbs]
            def finish(ss,b,kbs,p):
                if safe:
                    top=functools.reduce(jnp.maximum,[jnp.max(s,axis=0,keepdims=True) for s in ss])
                    ss=[s-top for s in ss]
                ps=[jnp.exp2(s).astype(bf) for s in ss]
                pc=jnp.concatenate(ps,axis=0) if len(ps)>1 else ps[0]
                vc=[v_ref[kb,p] for kb in kbs]
                vc=jnp.concatenate(vc,axis=1) if len(vc)>1 else vc[0]
                return mm(vc,pc)
            def emit(o,b,kbs,p):
                lanes=pl.ds(pl.multiple_of(b*128,128),128)
                den=o[64:72,:]
                inv=1.0/den[0:1]
                a_ref[p*64:p*64+32,lanes]=(o[0:32,:128]*inv[:,:128]).astype(bf)
                a_ref[p*64+32:p*64+64,lanes]=(o[32:64,128:]*inv[:,128:]).astype(bf)
                return den
            N=len(units); LA=N; LO=99
            pend={u:scores(*units[u]) for u in range(LA)}
            dens=[]; outs=[]
            for u in range(N):
                if u+LA<N: pend[u+LA]=scores(*units[u+LA])
                outs.append((u,finish(pend.pop(u),*units[u])))
                if len(outs)>LO:
                    v,o=outs.pop(0); dens.append(emit(o,*units[v]))
            for v,o in outs: dens.append(emit(o,*units[v]))
            if not safe:
                lim[0]=jnp.minimum(lim[0],functools.reduce(jnp.minimum,dens))
                lim[1]=jnp.maximum(lim[1],functools.reduce(jnp.maximum,dens))
        cnt=lambda b: ism[slot,0,12+b]
        lst=lambda b,c: [ism[slot,0,b*3+s] for s in range(c)]
        if True:
            def two(g,_):
                x=cnt(2*g); y=cnt(2*g+1)
                sw=(y>x).astype(jnp.int32)
                b0=2*g+sw; b1=2*g+1-sw
                hi=jnp.maximum(x,y); lo=jnp.minimum(x,y)
                for c0 in (1,2,3):
                    for c1 in range(1,c0+1):
                        pl.when((hi==c0)&(lo==c1))(lambda c0=c0,c1=c1: run([(b0,lst(b0,c0)),(b1,lst(b1,c1))]))
                return 0
            lax.fori_loop(0,2,two,0)
        else:
            def one(b,_):
                for c in (1,2,3):
                    pl.when(cnt(b)==c)(lambda c=c: run([(b,lst(b,c))]))
                return 0
            lax.fori_loop(0,4,one,0)

    C=2; T=A//C
    def ffn(l,then):
        cols=[slice(c*T,c*T+T) for c in range(C)]
        hs=[h_ref[:,s]+mm(wo[l],a_ref[:,s]) for s in cols]
        us=[mm(wu[l],norm(h,gn[2*l+1])) for h in hs]
        for c in range(C):
            u=us[c]
            z=u*(0.7978845608028654+0.035677408136300125*(u*u))
            half=0.5*u
            g=(half+half*jnp.tanh(z)).astype(bf)
            then(c,cols[c],hs[c]+mm(wd[l],g))
    def final(i,h,prev):
        r=rscale(h)
        res=[]
        for t in range(2):
            g=gr[t]
            acc=prev[t]
            for c in range(0,h.shape[1],128):
                acc=acc+jnp.sum(h[:,c:c+128]*g,axis=0,keepdims=True)*r[:,c:c+128]
            res.append(acc)
        return res

    def everything(safe):
        fetch(0); fetched(0)
        cp=ints(0); cp.start()
        fetch(1)
        for c in range(2):
            cs=slice(c*256,c*256+256)
            h=xbuf[0,0:D,cs].astype(f32)
            h_ref[:,cs]=h
            qkv(0,c,h)
        cp.wait()
        def config(i,_):
            s=lax.rem(i,2)
            def layer(l,_):
                attention(s,safe)
                @pl.when(l==0)
                def _():
                    def then(c,cs,h):
                        h_ref[:,cs]=h
                        qkv(1,c,h)
                    ffn(0,then)
                @pl.when(l==1)
                def _():
                    @pl.when(i+1<n)
                    def _():
                        fetched(i+1)
                        cp=ints(i+1); cp.start(); cp.wait()
                    o=1-s
                    accs=[[0.0,0.0]]
                    nxt=[xbuf[o,0:D,c*256:c*256+256].astype(f32) for c in range(2)]
                    for c in range(2): qkv(0,c,nxt[c])
                    def then(c,cs,h):
                        accs.append(final(i,h,accs[-1]))
                    ffn(1,then)
                    for c in range(2): h_ref[:,c*256:c*256+256]=nxt[c]
                    for t in range(2): out[t,pl.ds(i,1)]=accs[-1][t]
                    fetch(i+2)
                return 0
            lax.fori_loop(0,2,layer,0)
            return 0
        lax.fori_loop(0,n,config,0)
    lim[...]=jnp.full(lim.shape,1.0,f32)
    everything(False)
    good=(jnp.min(lim[0])>2.0**-80)&(jnp.max(lim[1])<2.0**100)
    pl.when(jnp.logical_not(good))(lambda: everything(True))


def evaluate(xs, ws):
    n = len(xs)
    V = pl.BlockSpec(memory_space=pltpu.VMEM)
    macs = n * 2 * (D * A * (3 * D + D + 4 * D) + 9 * 8 * B * B * 64)
    return pl.pallas_call(
        functools.partial(kernel, n),
        out_shape=jax.ShapeDtypeStruct((2, n, 128), f32),
        in_specs=[pl.BlockSpec(memory_space=pl.ANY)] * n + [V] * 6,
        out_specs=V,
        scratch_shapes=[
            pltpu.VMEM((2, D + EXTRA, A), bf),
            pltpu.VMEM((D, A), f32),
            pltpu.VMEM((NB, B, D), bf),
            pltpu.VMEM((NB, 4, 80, B), bf),
            pltpu.VMEM((NB, 4, 128, 256), bf),
            pltpu.VMEM((D, A), bf),
            pltpu.VMEM((2, 8, 256), f32),
            pltpu.VMEM((16, 128), jnp.int32),
            pltpu.SMEM((2, 16, 128), jnp.int32),
            pltpu.SemaphoreType.DMA((2,)),
            pltpu.SemaphoreType.DMA,
        ],
        compiler_params=pltpu.CompilerParams(vmem_limit_bytes=56 * 2**20),
        cost_estimate=pl.CostEstimate(flops=2 * macs, bytes_accessed=n * 278528, transcendentals=n * 2400000),
    )(*xs, *ws)


def solve_kernel(states, walks, *refs):
    parts = refs[: len(GROUPS)]
    pot, energy, mean, mat, rows, ssem, rsem, wssem, wrsem = refs[len(GROUPS) :]
    me, mw = lax.axis_index("state"), lax.axis_index("walk")
    barrier = pltpu.get_barrier_semaphore()
    for d in range(1, states):
        pl.semaphore_signal(barrier, inc=1, device_id=(lax.rem(me + d, states), mw), device_id_type=MESH)
    for d in range(1, walks):
        pl.semaphore_signal(barrier, inc=1, device_id=(me, lax.rem(mw + d, walks)), device_id_type=MESH)

    lane = lax.broadcasted_iota(jnp.int32, (states, 128), 1)
    row_at = lax.broadcasted_iota(jnp.int32, (states, 128), 0)
    config = jnp.bitwise_xor(row_at, me)

    def spread(t):
        whole = jnp.concatenate([p[t] for p in parts], axis=0)
        value = jnp.sum(whole, axis=1, keepdims=True)
        return jnp.sum(jnp.where(lane == config + t * 0, value, 0.0), axis=0, keepdims=True), jnp.sum(
            jnp.where(lane == config + states, value, 0.0), axis=0, keepdims=True
        )

    lane1 = lane[0:1]
    amp = spread(0)[1]
    ham = spread(1)[0]
    eye = jnp.where(lane1 == me + states, 1.0, 0.0)
    psi = jnp.where(lane1 < states, 0.0, eye + 0.9 / states * jnp.tanh(amp))
    mat[pl.ds(me, 1), :] = ham + jnp.where(lane1 < 2 * states, psi, 0.0)
    pl.semaphore_wait(barrier, states - 1 + walks - 1)

    def send(d):
        return pltpu.make_async_remote_copy(
            src_ref=mat.at[pl.ds(me, 1)], dst_ref=mat.at[pl.ds(me, 1)], send_sem=ssem.at[d], recv_sem=rsem.at[d],
            device_id=(lax.rem(me + d, states), mw), device_id_type=MESH,
        )

    for d in range(1, states):
        send(d).start()
    for d in range(1, states):
        came = lax.rem(me + states - d, states)
        pltpu.make_async_remote_copy(
            src_ref=mat.at[pl.ds(me, 1)], dst_ref=mat.at[pl.ds(came, 1)], send_sem=ssem.at[d], recv_sem=rsem.at[d],
            device_id=(lax.rem(me + d, states), mw), device_id_type=MESH,
        ).wait_recv()
    m = mat[...]
    for k in range(states):
        pivot_row = m[k : k + 1, :]
        scaled = pivot_row / pivot_row[:, states + k : states + k + 1]
        column = m[:, states + k : states + k + 1]
        m = jnp.where(row_at == k, scaled, m - column * scaled)
    mine = jnp.sum(jnp.where(row_at == me, m, 0.0), axis=0, keepdims=True)
    mine = jnp.where(lane1 == me, mine + pot[...], mine)
    energy[...] = mine[:, :states]
    rows[pl.ds(mw, 1), :] = mine

    def send_row(d):
        return pltpu.make_async_remote_copy(
            src_ref=rows.at[pl.ds(mw, 1)], dst_ref=rows.at[pl.ds(mw, 1)], send_sem=wssem.at[d], recv_sem=wrsem.at[d],
            device_id=(me, lax.rem(mw + d, walks)), device_id_type=MESH,
        )

    for d in range(1, walks):
        send_row(d).start()
    for d in range(1, walks):
        came = lax.rem(mw + walks - d, walks)
        pltpu.make_async_remote_copy(
            src_ref=rows.at[pl.ds(mw, 1)], dst_ref=rows.at[pl.ds(came, 1)], send_sem=wssem.at[d], recv_sem=wrsem.at[d],
            device_id=(me, lax.rem(mw + d, walks)), device_id_type=MESH,
        ).wait_recv()
    mean[...] = (jnp.sum(rows[...], axis=0, keepdims=True) * (1.0 / walks))[:, :states]
    for d in range(1, states):
        send(d).wait_send()
    for d in range(1, walks):
        send_row(d).wait_send()


def solve(parts, potential, states, walks):
    V = pl.BlockSpec(memory_space=pltpu.VMEM)
    dma = pltpu.SemaphoreType.DMA
    return pl.pallas_call(
        functools.partial(solve_kernel, states, walks),
        out_shape=(jax.ShapeDtypeStruct((1, states), f32), jax.ShapeDtypeStruct((1, states), f32)),
        in_specs=[V] * (len(parts) + 1),
        out_specs=(V, V),
        scratch_shapes=[
            pltpu.VMEM((states, 128), f32),
            pltpu.VMEM((walks, 128), f32),
            dma((states,)), dma((states,)), dma((walks,)), dma((walks,)),
        ],
        compiler_params=pltpu.CompilerParams(collective_id=0, has_side_effects=True),
    )(*parts, potential)


def local(features, key_blocks, block_counts, potential, w_qkv, w_out, w_up, w_down, gains, readouts):
    states, walks = lax.axis_size("state"), lax.axis_size("walk")
    ints = jnp.concatenate([key_blocks.reshape(-1), block_counts.reshape(-1)]).astype(bf)
    extra = jnp.pad(ints[None], ((0, EXTRA - 1), (0, A - ints.shape[0])))
    mine = jnp.concatenate([features[0, 0].T, extra], axis=0)
    xs = [mine] + [lax.ppermute(mine, "state", [(s, s ^ k) for s in range(states)]) for k in range(1, states)]
    g = gains[0]
    ws = (
        w_qkv[0].swapaxes(1, 2),
        w_out[0].swapaxes(1, 2),
        w_up[0].swapaxes(1, 2),
        w_down[0].swapaxes(1, 2),
        jnp.broadcast_to(g[0:4, :, None], (4, D, 128)),
        jnp.broadcast_to((g[4] * readouts[0] / jnp.sqrt(f32(A)))[:, :, None], (2, D, 128)),
    )
    parts, at = [], 0
    for n in GROUPS:
        parts.append(evaluate(xs[at : at + n], ws))
        at += n
    energy, mean = solve(parts, potential, states, walks)
    return energy[:, :, None], mean


def solution(mesh):
    placed = (
        P("state", "walk", None, None),
        P("state", "walk", None, None),
        P("state", "walk", None),
        P("state", "walk"),
        P("state", None, None, None),
        P("state", None, None, None),
        P("state", None, None, None),
        P("state", None, None, None),
        P("state", None, None),
        P("state", None, None),
    )
    return jax.shard_map(
        local,
        mesh=mesh,
        in_specs=placed,
        out_specs=(P("state", None, "walk"), P("state", None)),
        check_vma=False,
    )
```

```python
import functools

import jax
import jax.numpy as jnp
from jax import lax
from jax.experimental import pallas as pl
from jax.experimental.pallas import tpu as pltpu
from jax.sharding import PartitionSpec as P

D = 256
A = 512
B = 128
NB = 4
H = 8
SLOTS = 3
EXTRA = 16
EARLY = 4
QS = 1.4426950408889634 / 32.0**0.5
bf = jnp.bfloat16
f32 = jnp.float32
MESH = pl.DeviceIdType.MESH
V = pl.BlockSpec(memory_space=pltpu.VMEM)
ANY = pl.BlockSpec(memory_space=pl.ANY)


def mm(a, b):
    return lax.dot_general(a, b, (((1,), (0,)), ((), ())), preferred_element_type=f32)


def rscale(h):
    return lax.rsqrt(jnp.sum(h * h, axis=0, keepdims=True) * (1.0 / D) + 1e-6)


def norm(h, g):
    r = rscale(h)
    parts = [((h[:, c : c + 128] * r[:, c : c + 128]) * g).astype(bf) for c in range(0, h.shape[1], 128)]
    return jnp.concatenate(parts, axis=1)


class Net:
    def __init__(self, weights, scratch):
        self.wqkv, self.wo, self.wu, self.wd, self.gn, self.gr = weights
        self.h, self.k, self.v, self.qx, self.a, self.lim, self.ivm, self.ism, self.isem, self.xbuf, self.xsem = scratch

    def clear(self):
        self.qx[...] = jnp.zeros(self.qx.shape, bf)
        self.v[...] = jnp.ones(self.v.shape, bf)
        self.lim[...] = jnp.ones(self.lim.shape, f32)

    def ints(self, s):
        self.ivm[...] = self.xbuf[s, D : D + EXTRA, 0:128].astype(f32).astype(jnp.int32)
        return pltpu.make_async_copy(self.ivm, self.ism.at[s], self.isem)

    def project(self, l, c, h):
        n = norm(h, self.gn[2 * l])
        q = (mm(self.wqkv[l, 0:256, :], n) * QS).astype(bf)
        k = mm(self.wqkv[l, 256:512, :], n).astype(bf).T
        v = mm(self.wqkv[l, 512:768, :], n).astype(bf)
        for head in range(H):
            row, lane = (head % 4) * 32, (head % 2) * 128
            for b in range(2):
                self.qx[2 * c + b, head // 2, row : row + 32, lane : lane + 128] = q[
                    head * 32 : head * 32 + 32, b * 128 : b * 128 + 128
                ]
        for b in range(2):
            self.k[2 * c + b] = k[b * 128 : b * 128 + 128, :]
            for p in range(4):
                self.v[2 * c + b, p, 0:64, :] = v[p * 64 : p * 64 + 64, b * 128 : b * 128 + 128]

    def scores(self, b, kbs, p):
        half = p // 2 * 128
        return [mm(self.k[kb, :, half : half + 128], self.qx[b, p]) for kb in kbs]

    def mix(self, ss, kbs, p, keep, safe):
        if safe:
            top = functools.reduce(jnp.maximum, [jnp.max(s, axis=0, keepdims=True) for s in ss])
            ss = [s - top for s in ss]
        ps = [jnp.exp2(s).astype(bf) for s in ss]
        if keep is not None:
            ps = [jnp.where(ok, q, jnp.zeros_like(q)) if s else q for s, (ok, q) in enumerate(zip(keep, ps))]
        vs = [self.v[kb, p] for kb in kbs]
        return mm(jnp.concatenate(vs, axis=1), jnp.concatenate(ps, axis=0))

    def emit(self, o, b, p):
        den = o[64:72, :]
        inv = 1.0 / den[0:1]
        lanes = pl.ds(pl.multiple_of(b * 128, 128), 128)
        self.a[p * 64 : p * 64 + 32, lanes] = (o[0:32, :128] * inv[:, :128]).astype(bf)
        self.a[p * 64 + 32 : p * 64 + 64, lanes] = (o[32:64, 128:] * inv[:, 128:]).astype(bf)
        return den

    def attend(self, items, safe):
        units = [(b, kbs, keep, p) for p in range(4) for b, kbs, keep in items]
        ss = [self.scores(b, kbs, p) for b, kbs, _, p in units]
        outs = [self.mix(s, kbs, p, keep, safe) for s, (_, kbs, keep, p) in zip(ss, units)]
        dens = [self.emit(o, b, p) for o, (b, _, _, p) in zip(outs, units)]
        if not safe:
            self.lim[0] = jnp.minimum(self.lim[0], functools.reduce(jnp.minimum, dens))
            self.lim[1] = jnp.maximum(self.lim[1], functools.reduce(jnp.maximum, dens))

    def attention_masked(self, s):
        def two(g, _):
            items = []
            for b in (2 * g, 2 * g + 1):
                count = self.ism[s, 0, SLOTS * NB + b]
                kbs = [jnp.clip(self.ism[s, 0, b * SLOTS + t], 0, NB - 1) for t in range(SLOTS)]
                items.append((b, kbs, [count > t for t in range(SLOTS)]))
            self.attend(items, False)
            return 0

        lax.fori_loop(0, NB // 2, two, 0)

    def attention(self, s, safe):
        def two(g, _):
            x, y = self.ism[s, 0, SLOTS * NB + 2 * g], self.ism[s, 0, SLOTS * NB + 2 * g + 1]
            swap = (y > x).astype(jnp.int32)
            more, less = 2 * g + swap, 2 * g + 1 - swap
            most, least = jnp.maximum(x, y), jnp.minimum(x, y)

            def run(c0, c1):
                lists = [(b, [self.ism[s, 0, b * SLOTS + t] for t in range(c)], None) for b, c in ((more, c0), (less, c1))]
                self.attend(lists, safe)

            for c0 in range(1, SLOTS + 1):
                for c1 in range(1, c0 + 1):
                    pl.when((most == c0) & (least == c1))(functools.partial(run, c0, c1))
            return 0

        lax.fori_loop(0, NB // 2, two, 0)

    def feed(self, l, then):
        cols = [slice(c * 256, c * 256 + 256) for c in range(2)]
        hs = [self.h[:, s] + mm(self.wo[l], self.a[:, s]) for s in cols]
        us = [mm(self.wu[l], norm(h, self.gn[2 * l + 1])) for h in hs]
        for c in range(2):
            u = us[c]
            z = u * (0.7978845608028654 + 0.035677408136300125 * (u * u))
            half = 0.5 * u
            g = (half + half * jnp.tanh(z)).astype(bf)
            then(c, hs[c] + mm(self.wd[l], g))

    def final(self, h, sums):
        r = rscale(h)
        out = []
        for t in range(2):
            g, acc = self.gr[t], sums[t]
            for c in range(0, h.shape[1], 128):
                acc = acc + jnp.sum(h[:, c : c + 128] * g, axis=0, keepdims=True) * r[:, c : c + 128]
            out.append(acc)
        return out

    def run(self, first, count, attention, fetch, out, at, between=None):
        def begin(s):
            return [self.xbuf[s, 0:D, c * 256 : c * 256 + 256].astype(f32) for c in range(2)]

        s0 = first % 2
        fetch(first).start()
        fetch(first).wait()
        lists = self.ints(s0)
        lists.start()
        for c, h in enumerate(begin(s0)):
            self.h[:, c * 256 : c * 256 + 256] = h
            self.project(0, c, h)
        lists.wait()

        def config(i, _):
            s = lax.rem(i, 2)
            if between is not None:
                between(i)

            @pl.when(i + 1 < first + count)
            def _():
                fetch(i + 1).start()

            def layer(l, _):
                attention(s)

                @pl.when(l == 0)
                def _():
                    def then(c, h):
                        self.h[:, c * 256 : c * 256 + 256] = h
                        self.project(1, c, h)

                    self.feed(0, then)

                @pl.when(l == 1)
                def _():
                    @pl.when(i + 1 < first + count)
                    def _():
                        fetch(i + 1).wait()
                        lists = self.ints(1 - s)
                        lists.start()
                        lists.wait()

                    sums = [[0.0, 0.0]]
                    later = begin(1 - s)
                    for c in range(2):
                        self.project(0, c, later[c])
                    self.feed(1, lambda c, h: sums.append(self.final(h, sums[-1])))
                    for c in range(2):
                        self.h[:, c * 256 : c * 256 + 256] = later[c]
                    for t in range(2):
                        out[t, pl.ds(i - at, 1)] = sums[-1][t]

                return 0

            lax.fori_loop(0, 2, layer, 0)
            return 0

        lax.fori_loop(first, first + count, config, 0)


def scratch():
    return [
        pltpu.VMEM((D, A), f32),
        pltpu.VMEM((NB, B, D), bf),
        pltpu.VMEM((NB, 4, 80, B), bf),
        pltpu.VMEM((NB, 4, B, 2 * B), bf),
        pltpu.VMEM((D, A), bf),
        pltpu.VMEM((2, 8, 2 * B), f32),
        pltpu.VMEM((EXTRA, 128), jnp.int32),
        pltpu.SMEM((2, EXTRA, 128), jnp.int32),
        pltpu.SemaphoreType.DMA,
        pltpu.VMEM((2, D + EXTRA, A), bf),
        pltpu.SemaphoreType.DMA((2,)),
    ]


def flip(me, k):
    out = 0
    for bit in (1, 2, 4, 8):
        mine = lax.rem(lax.div(me, bit), 2)
        out = out + bit * ((1 - mine) if k & bit else mine)
    return out


def gather_kernel(states, x_ref, *refs):
    weights, (all_ref, out, lims) = refs[:6], refs[6:9]
    net = Net(weights, refs[9:20])
    ssem, rsem, csem = refs[20:]
    me, mw = lax.axis_index("state"), lax.axis_index("walk")
    barrier = pltpu.get_barrier_semaphore()
    partners = [1] + list(range(2, states, 2))
    for k in partners:
        pl.semaphore_signal(barrier, inc=1, device_id=(flip(me, k), mw), device_id_type=MESH)
    own = pltpu.make_async_copy(x_ref, all_ref.at[0], csem)
    own.start()
    net.clear()
    pl.semaphore_wait(barrier, len(partners))

    def send(k):
        return pltpu.make_async_remote_copy(
            src_ref=x_ref, dst_ref=all_ref.at[k], send_sem=ssem.at[k], recv_sem=rsem.at[k],
            device_id=(flip(me, k), mw), device_id_type=MESH,
        )

    def relay(k):
        return pltpu.make_async_remote_copy(
            src_ref=all_ref.at[k], dst_ref=all_ref.at[k + 1], send_sem=ssem.at[k + 1], recv_sem=rsem.at[k + 1],
            device_id=(flip(me, 1), mw), device_id_type=MESH,
        )

    order = [1] + [k for k in ORDER if k < states]
    for k in order:
        send(k).start()
    own.wait()

    def fetch(i):
        s = lax.rem(i, 2)
        return pltpu.make_async_copy(all_ref.at[i], net.xbuf.at[s], net.xsem.at[s])

    def between(i):
        for n in range(EARLY):
            @pl.when(i == n)
            def _():
                if n + 1 < EARLY:
                    if n == 0:
                        send(1).wait_recv()
                    if n == 1:
                        send(2).wait_recv()
                        relay(2).start()
                    if n == 2:
                        relay(2).wait_recv()
                for k in BEFORE[n]:
                    send(k).wait_recv()
                    relay(k).start()

    net.run(0, EARLY, net.attention_masked, fetch, out, 0, between)
    done = {2} | {k for ks in BEFORE for k in ks}
    for k in order[1:]:
        if k not in done:
            send(k).wait_recv()
            relay(k).start()
    for k in order[1:]:
        if k != 2:
            relay(k).wait_recv()
    for k in order:
        send(k).wait_send()
    for k in order[1:]:
        relay(k).wait_send()
    lims[...] = net.lim[...]


ORDER = (2, 4, 12, 6, 14, 8, 10)
BEFORE = ((), (), (4, 12), (6, 14))


def gather(x, ws, states):
    return pl.pallas_call(
        functools.partial(gather_kernel, states),
        out_shape=(
            jax.ShapeDtypeStruct((states, D + EXTRA, A), bf),
            jax.ShapeDtypeStruct((2, EARLY, 128), f32),
            jax.ShapeDtypeStruct((2, 8, 2 * B), f32),
        ),
        in_specs=[ANY] + [V] * 6,
        out_specs=(ANY, V, V),
        scratch_shapes=scratch()
        + [pltpu.SemaphoreType.DMA((states,)), pltpu.SemaphoreType.DMA((states,)), pltpu.SemaphoreType.DMA],
        compiler_params=pltpu.CompilerParams(collective_id=1, has_side_effects=True, vmem_limit_bytes=56 * 2**20),
    )(x, *ws)


def rest_kernel(states, all_ref, early, lims, *refs):
    weights, out = refs[:6], refs[6]
    net = Net(weights, refs[7:])
    net.clear()

    def fetch(i):
        s = lax.rem(i, 2)
        return pltpu.make_async_copy(all_ref.at[i], net.xbuf.at[s], net.xsem.at[s])

    def within(lim):
        return (jnp.min(lim[0]) > 2.0**-80) & (jnp.max(lim[1]) < 2.0**100)

    out[:, 0:EARLY] = early[...]
    net.run(EARLY, states - EARLY, lambda s: net.attention(s, False), fetch, out, 0)

    @pl.when(jnp.logical_not(within(lims) & within(net.lim)))
    def _():
        net.run(0, states, lambda s: net.attention(s, True), fetch, out, 0)


def rest(every, early, lims, ws, states):
    return pl.pallas_call(
        functools.partial(rest_kernel, states),
        out_shape=jax.ShapeDtypeStruct((2, states, 128), f32),
        in_specs=[ANY] + [V] * 8,
        out_specs=V,
        scratch_shapes=scratch(),
        compiler_params=pltpu.CompilerParams(vmem_limit_bytes=56 * 2**20),
    )(every, early, lims, *ws)


def solve_kernel(states, walks, *refs):
    parts, pot, energy, mean, mat, rows, ssem, rsem, wssem, wrsem = refs
    me, mw = lax.axis_index("state"), lax.axis_index("walk")
    barrier = pltpu.get_barrier_semaphore()
    for d in range(1, states):
        pl.semaphore_signal(barrier, inc=1, device_id=(lax.rem(me + d, states), mw), device_id_type=MESH)
    for d in range(1, walks):
        pl.semaphore_signal(barrier, inc=1, device_id=(me, lax.rem(mw + d, walks)), device_id_type=MESH)

    lane = lax.broadcasted_iota(jnp.int32, (states, 128), 1)
    row_at = lax.broadcasted_iota(jnp.int32, (states, 128), 0)
    config = jnp.bitwise_xor(row_at, me)

    def spread(t):
        value = jnp.sum(parts[t], axis=1, keepdims=True)
        return jnp.sum(jnp.where(lane == config + (1 - t) * states, value, 0.0), axis=0, keepdims=True)

    lane1 = lane[0:1]
    amp = spread(0)
    ham = spread(1)
    eye = jnp.where(lane1 == me + states, 1.0, 0.0)
    psi = jnp.where(lane1 < states, 0.0, eye + 0.9 / states * jnp.tanh(amp))
    mat[pl.ds(me, 1), :] = ham + jnp.where(lane1 < 2 * states, psi, 0.0)
    pl.semaphore_wait(barrier, states - 1 + walks - 1)

    def send(d):
        return pltpu.make_async_remote_copy(
            src_ref=mat.at[pl.ds(me, 1)], dst_ref=mat.at[pl.ds(me, 1)], send_sem=ssem.at[d], recv_sem=rsem.at[d],
            device_id=(lax.rem(me + d, states), mw), device_id_type=MESH,
        )

    for d in range(1, states):
        send(d).start()
    for d in range(1, states):
        came = lax.rem(me + states - d, states)
        pltpu.make_async_remote_copy(
            src_ref=mat.at[pl.ds(me, 1)], dst_ref=mat.at[pl.ds(came, 1)], send_sem=ssem.at[d], recv_sem=rsem.at[d],
            device_id=(lax.rem(me + d, states), mw), device_id_type=MESH,
        ).wait_recv()
    m = mat[...]
    for k in range(states):
        pivot_row = m[k : k + 1, :]
        scaled = pivot_row / pivot_row[:, states + k : states + k + 1]
        column = m[:, states + k : states + k + 1]
        m = jnp.where(row_at == k, scaled, m - column * scaled)
    mine = jnp.sum(jnp.where(row_at == me, m, 0.0), axis=0, keepdims=True)
    mine = jnp.where(lane1 == me, mine + pot[...], mine)
    energy[...] = mine[:, :states]
    rows[pl.ds(mw, 1), :] = mine

    def send_row(d):
        return pltpu.make_async_remote_copy(
            src_ref=rows.at[pl.ds(mw, 1)], dst_ref=rows.at[pl.ds(mw, 1)], send_sem=wssem.at[d], recv_sem=wrsem.at[d],
            device_id=(me, lax.rem(mw + d, walks)), device_id_type=MESH,
        )

    for d in range(1, walks):
        send_row(d).start()
    for d in range(1, walks):
        came = lax.rem(mw + walks - d, walks)
        pltpu.make_async_remote_copy(
            src_ref=rows.at[pl.ds(mw, 1)], dst_ref=rows.at[pl.ds(came, 1)], send_sem=wssem.at[d], recv_sem=wrsem.at[d],
            device_id=(me, lax.rem(mw + d, walks)), device_id_type=MESH,
        ).wait_recv()
    mean[...] = (jnp.sum(rows[...], axis=0, keepdims=True) * (1.0 / walks))[:, :states]
    for d in range(1, states):
        send(d).wait_send()
    for d in range(1, walks):
        send_row(d).wait_send()


def solve(parts, potential, states, walks):
    dma = pltpu.SemaphoreType.DMA
    return pl.pallas_call(
        functools.partial(solve_kernel, states, walks),
        out_shape=(jax.ShapeDtypeStruct((1, states), f32), jax.ShapeDtypeStruct((1, states), f32)),
        in_specs=[V, V],
        out_specs=(V, V),
        scratch_shapes=[
            pltpu.VMEM((states, 128), f32),
            pltpu.VMEM((walks, 128), f32),
            dma((states,)), dma((states,)), dma((walks,)), dma((walks,)),
        ],
        compiler_params=pltpu.CompilerParams(collective_id=0, has_side_effects=True),
    )(parts, potential)


def local(features, key_blocks, block_counts, potential, w_qkv, w_out, w_up, w_down, gains, readouts):
    states, walks = lax.axis_size("state"), lax.axis_size("walk")
    ints = jnp.concatenate([key_blocks.reshape(-1), block_counts.reshape(-1)]).astype(bf)
    extra = jnp.pad(ints[None], ((0, EXTRA - 1), (0, A - ints.shape[0])))
    mine = jnp.concatenate([features[0, 0].T, extra], axis=0)
    g = gains[0]
    ws = (
        w_qkv[0].swapaxes(1, 2),
        w_out[0].swapaxes(1, 2),
        w_up[0].swapaxes(1, 2),
        w_down[0].swapaxes(1, 2),
        jnp.broadcast_to(g[0:4, :, None], (4, D, 128)),
        jnp.broadcast_to((g[4] * readouts[0] / jnp.sqrt(f32(A)))[:, :, None], (2, D, 128)),
    )
    every, early, lims = gather(mine, ws, states)
    parts = rest(every, early, lims, ws, states)
    energy, mean = solve(parts, potential, states, walks)
    return energy[:, :, None], mean


def solution(mesh):
    placed = (
        P("state", "walk", None, None),
        P("state", "walk", None, None),
        P("state", "walk", None),
        P("state", "walk"),
        P("state", None, None, None),
        P("state", None, None, None),
        P("state", None, None, None),
        P("state", None, None, None),
        P("state", None, None),
        P("state", None, None),
    )
    return jax.shard_map(
        local,
        mesh=mesh,
        in_specs=placed,
        out_specs=(P("state", None, "walk"), P("state", None)),
        check_vma=False,
    )
```

```python
import functools
import itertools

import jax
import jax.numpy as jnp
from jax import lax
from jax.experimental import pallas as pl
from jax.experimental.pallas import tpu as pltpu
from jax.sharding import PartitionSpec as P

D = 256
A = 512
B = 128
NB = 4
H = 8
SLOTS = 3
EXTRA = 16
COUNTS = 8
EARLY = 6
AHEAD = 8
OFFSETS = (0, 1, 4, 5, 12, 13, 2, 3, 6, 7, 14, 15, 8, 9, 10, 11)
WAVES = ((1, 2, 4, 6), (8, 10, 12), (14,))
BEFORE = ((), (2,), (4,), (6,), (8,), (10, 12))
QS = 1.4426950408889634 / 32.0**0.5
bf = jnp.bfloat16
f32 = jnp.float32
MESH = pl.DeviceIdType.MESH
V = pl.BlockSpec(memory_space=pltpu.VMEM)
ANY = pl.BlockSpec(memory_space=pl.ANY)


def mm(a, b):
    return lax.dot_general(a, b, (((1,), (0,)), ((), ())), preferred_element_type=f32)


def rscale(h):
    return lax.rsqrt(jnp.sum(h * h, axis=0, keepdims=True) * (1.0 / D) + 1e-6)


def norm(h, g):
    r = rscale(h)
    parts = [((h[:, c : c + 128] * r[:, c : c + 128]) * g).astype(bf) for c in range(0, h.shape[1], 128)]
    return jnp.concatenate(parts, axis=1)


class Net:
    def __init__(self, weights, scratch):
        self.raw = weights
        self.wqkv, self.wo, self.wu, self.wd, self.gn, self.gr = scratch[:6]
        self.h, self.k, self.v, self.qx, self.a, self.lim = scratch[6:12]
        self.ivm, self.ism, self.isem, self.xbuf, self.xsem = scratch[12:]

    def clear(self):
        self.qx[...] = jnp.zeros(self.qx.shape, bf)
        self.v[...] = jnp.ones(self.v.shape, bf)
        self.lim[...] = jnp.ones(self.lim.shape, f32)

    def prepare(self):
        *mats, gains, readouts = self.raw

        def layer(l, _):
            for w, t in zip(mats, (self.wqkv, self.wo, self.wu, self.wd)):
                for r in range(0, w.shape[1], 256):
                    for c in range(0, w.shape[2], 256):
                        tile = w[l, r : r + 256, c : c + 256].T
                        t[l, c : c + 256, r : r + 256] = tile * bf(0.5) if t is self.wd else tile
            return 0

        lax.fori_loop(0, 2, layer, 0)

        def column(row):
            return jnp.broadcast_to(row, (128, D)).T

        for r in range(4):
            self.gn[r] = column(gains[r : r + 1, :])
        last = gains[4:5, :] * (1.0 / A**0.5)
        for t in range(2):
            self.gr[t] = column(last * readouts[t : t + 1, :])

    def ints(self, s):
        self.ivm[...] = self.xbuf[s, D : D + EXTRA, 0:128].astype(f32).astype(jnp.int32)
        return pltpu.make_async_copy(self.ivm, self.ism.at[s], self.isem)

    def project(self, l, c, h):
        n = norm(h, self.gn[2 * l])
        q = (mm(self.wqkv[l, 0:256, :], n) * QS).astype(bf)
        k = mm(self.wqkv[l, 256:512, :], n).astype(bf).T
        v = mm(self.wqkv[l, 512:768, :], n).astype(bf)
        for head in range(H):
            row, lane = (head % 4) * 32, (head % 2) * 128
            for b in range(2):
                self.qx[2 * c + b, head // 2, row : row + 32, lane : lane + 128] = q[
                    head * 32 : head * 32 + 32, b * 128 : b * 128 + 128
                ]
        for b in range(2):
            self.k[2 * c + b] = k[b * 128 : b * 128 + 128, :]
            for p in range(4):
                self.v[2 * c + b, p, 0:64, :] = v[p * 64 : p * 64 + 64, b * 128 : b * 128 + 128]

    def scores(self, b, kbs, p):
        half = p // 2 * 128
        return [mm(self.k[kb, :, half : half + 128], self.qx[b, p]) for kb in kbs]

    def mix(self, ss, kbs, p, keep, safe):
        if safe:
            top = functools.reduce(jnp.maximum, [jnp.max(s, axis=0, keepdims=True) for s in ss])
            ss = [s - top for s in ss]
        ps = [jnp.exp2(s).astype(bf) for s in ss]
        if keep is not None:
            ps = [jnp.where(ok, q, jnp.zeros_like(q)) if s else q for s, (ok, q) in enumerate(zip(keep, ps))]
        vs = [self.v[kb, p] for kb in kbs]
        return mm(jnp.concatenate(vs, axis=1), jnp.concatenate(ps, axis=0))

    def emit(self, o, b, p):
        den = o[64:72, :]
        inv = 1.0 / den[0:1]
        lanes = pl.ds(b * 128 if isinstance(b, int) else pl.multiple_of(b * 128, 128), 128)
        self.a[p * 64 : p * 64 + 32, lanes] = (o[0:32, :128] * inv[:, :128]).astype(bf)
        self.a[p * 64 + 32 : p * 64 + 64, lanes] = (o[32:64, 128:] * inv[:, 128:]).astype(bf)
        return den

    def attend(self, items, safe):
        units = [(b, kbs, keep, p) for b, kbs, keep in items for p in range(4)]
        ss = [self.scores(b, kbs, p) for b, kbs, _, p in units[:AHEAD]]
        dens = []
        for n, (b, kbs, keep, p) in enumerate(units):
            if n + AHEAD < len(units):
                later = units[n + AHEAD]
                ss.append(self.scores(later[0], later[1], later[3]))
            dens.append(self.emit(self.mix(ss[n], kbs, p, keep, safe), b, p))
        if not safe:
            self.lim[0] = jnp.minimum(self.lim[0], functools.reduce(jnp.minimum, dens))
            self.lim[1] = jnp.maximum(self.lim[1], functools.reduce(jnp.maximum, dens))

    def attention_masked(self, s):
        items = []
        for b in range(NB):
            count = self.ism[s, COUNTS, b]
            kbs = [jnp.clip(self.ism[s, b, t], 0, NB - 1) for t in range(SLOTS)]
            items.append((b, kbs, [count > t for t in range(SLOTS)]))
        self.attend(items, False)

    def attention(self, s, safe):
        count = [self.ism[s, COUNTS, b] for b in range(1, NB)]
        block = [jnp.int32(b) for b in range(1, NB)]
        for x, y in ((0, 1), (1, 2), (0, 1)):
            swap = count[y] > count[x]
            for seq in (count, block):
                seq[x], seq[y] = jnp.where(swap, seq[y], seq[x]), jnp.where(swap, seq[x], seq[y])
        for case in itertools.combinations_with_replacement(range(SLOTS, 0, -1), NB - 1):

            @pl.when((count[0] == case[0]) & (count[1] == case[1]) & (count[2] == case[2]))
            def _(case=case):
                todo = zip([0, *block], (SLOTS, *case))
                self.attend([(b, [self.ism[s, b, t] for t in range(c)], None) for b, c in todo], safe)

    def feed(self, l, then):
        h = self.h[...] + mm(self.wo[l], self.a[...])
        u = mm(self.wu[l], norm(h, self.gn[2 * l + 1]))
        z = u * (0.7978845608028654 + 0.035677408136300125 * (u * u))
        h = h + mm(self.wd[l], (u + u * jnp.tanh(z)).astype(bf))
        for c in range(2):
            then(c, h[:, c * 256 : c * 256 + 256])

    def final(self, h, sums):
        r = rscale(h)
        out = []
        for t in range(2):
            g, acc = self.gr[t], sums[t]
            for c in range(0, h.shape[1], 128):
                acc = acc + jnp.sum(h[:, c : c + 128] * g, axis=0, keepdims=True) * r[:, c : c + 128]
            out.append(acc)
        return out

    def run(self, first, count, attention, fetch, out, at, between=None):
        def begin(s):
            return [self.xbuf[s, 0:D, c * 256 : c * 256 + 256].astype(f32) for c in range(2)]

        s0 = first % 2
        fetch(first).start()
        fetch(first).wait()
        lists = self.ints(s0)
        lists.start()
        for c, h in enumerate(begin(s0)):
            self.h[:, c * 256 : c * 256 + 256] = h
            self.project(0, c, h)
        lists.wait()

        def config(i, _):
            s = lax.rem(i, 2)
            if between is not None:
                between(i)

            @pl.when(i + 1 < first + count)
            def _():
                fetch(i + 1).start()

            def layer(l, _):
                attention(s)

                @pl.when(l == 0)
                def _():
                    @pl.when(i + 1 < first + count)
                    def _():
                        fetch(i + 1).wait()
                        self.ints(1 - s).start()

                    def then(c, h):
                        self.h[:, c * 256 : c * 256 + 256] = h
                        self.project(1, c, h)

                    self.feed(0, then)

                @pl.when(l == 1)
                def _():
                    sums = [[0.0, 0.0]]
                    later = begin(1 - s)
                    for c in range(2):
                        self.project(0, c, later[c])
                    self.feed(1, lambda c, h: sums.append(self.final(h, sums[-1])))
                    for c in range(2):
                        self.h[:, c * 256 : c * 256 + 256] = later[c]
                    for t in range(2):
                        out[t, pl.ds(i - at, 1)] = sums[-1][t]

                    @pl.when(i + 1 < first + count)
                    def _():
                        pltpu.make_async_copy(self.ivm, self.ism.at[1 - s], self.isem).wait()

                return 0

            lax.fori_loop(0, 2, layer, 0)
            return 0

        lax.fori_loop(first, first + count, config, 0)


def scratch():
    return [
        pltpu.VMEM((2, 3 * D, D), bf),
        pltpu.VMEM((2, D, D), bf),
        pltpu.VMEM((2, 2 * D, D), bf),
        pltpu.VMEM((2, D, 2 * D), bf),
        pltpu.VMEM((4, D, 128), f32),
        pltpu.VMEM((2, D, 128), f32),
        pltpu.VMEM((D, A), f32),
        pltpu.VMEM((NB, B, D), bf),
        pltpu.VMEM((NB, 4, 80, B), bf),
        pltpu.VMEM((NB, 4, B, 2 * B), bf),
        pltpu.VMEM((D, A), bf),
        pltpu.VMEM((2, 8, 2 * B), f32),
        pltpu.VMEM((EXTRA, 128), jnp.int32),
        pltpu.SMEM((2, EXTRA, 128), jnp.int32),
        pltpu.SemaphoreType.DMA,
        pltpu.VMEM((2, D + EXTRA, A), bf),
        pltpu.SemaphoreType.DMA((2,)),
    ]


def flip(me, k):
    out = 0
    for bit in (1, 2, 4, 8):
        mine = lax.rem(lax.div(me, bit), 2)
        out = out + bit * ((1 - mine) if k & bit else mine)
    return out


def gather_kernel(states, feats, lists, counts, *refs):
    weights, (all_ref, out, lims) = refs[:6], refs[6:9]
    net = Net(weights, refs[9:26])
    x_ref, ssem, rsem, csem = refs[26:]
    me, mw = lax.axis_index("state"), lax.axis_index("walk")
    barrier = pltpu.get_barrier_semaphore()
    partners = [1] + list(range(2, states, 2))
    for k in partners:
        pl.semaphore_signal(barrier, inc=1, device_id=(flip(me, OFFSETS[k]), mw), device_id_type=MESH)
    x_ref[0:D, :] = feats[...].T
    net.ivm[...] = jnp.zeros(net.ivm.shape, jnp.int32)
    net.ivm[0:NB, 0:SLOTS] = lists[...]
    net.ivm[COUNTS : COUNTS + 1, 0:NB] = counts[...]
    x_ref[D : D + EXTRA, :] = jnp.zeros((EXTRA, A), bf)
    x_ref[D : D + EXTRA, 0:128] = net.ivm[...].astype(f32).astype(bf)
    own = pltpu.make_async_copy(x_ref, all_ref.at[0], csem)
    own.start()
    pl.semaphore_wait(barrier, len(partners))

    def send(k):
        return pltpu.make_async_remote_copy(
            src_ref=x_ref, dst_ref=all_ref.at[k], send_sem=ssem.at[k], recv_sem=rsem.at[k],
            device_id=(flip(me, OFFSETS[k]), mw), device_id_type=MESH,
        )

    def relay(k):
        return pltpu.make_async_remote_copy(
            src_ref=all_ref.at[k], dst_ref=all_ref.at[k + 1], send_sem=ssem.at[k + 1], recv_sem=rsem.at[k + 1],
            device_id=(flip(me, 1), mw), device_id_type=MESH,
        )

    def landed(k):
        send(k).wait_recv()
        if k > 1:
            relay(k).start()

    for k in WAVES[0]:
        send(k).start()
    net.clear()
    net.prepare()
    own.wait()

    def fetch(i):
        s = lax.rem(i, 2)
        return pltpu.make_async_copy(all_ref.at[i], net.xbuf.at[s], net.xsem.at[s])

    def between(i):
        for n in range(EARLY):

            @pl.when(i == n)
            def _(n=n):
                for k in WAVES[n + 1] if n + 1 < len(WAVES) else ():
                    send(k).start()
                if n == 0:
                    landed(1)
                for k in BEFORE[n]:
                    landed(k)
                if n % 2 == 0 and 0 < n < EARLY - 1:
                    relay(n).wait_recv()

    net.run(0, EARLY, net.attention_masked, fetch, out, 0, between)
    for k in partners[1:]:
        if all(k not in ks for ks in BEFORE):
            landed(k)
    for k in partners[1:]:
        if k + 1 >= EARLY:
            relay(k).wait_recv()
    for k in partners:
        send(k).wait_send()
    for k in partners[1:]:
        relay(k).wait_send()
    lims[...] = net.lim[...]


def gather(feats, lists, counts, ws, states):
    return pl.pallas_call(
        functools.partial(gather_kernel, states),
        out_shape=(
            jax.ShapeDtypeStruct((states, D + EXTRA, A), bf),
            jax.ShapeDtypeStruct((2, EARLY, 128), f32),
            jax.ShapeDtypeStruct((2, 8, 2 * B), f32),
        ),
        in_specs=[V] * 9,
        out_specs=(ANY, V, V),
        scratch_shapes=scratch()
        + [pltpu.VMEM((D + EXTRA, A), bf)]
        + [pltpu.SemaphoreType.DMA((states,)), pltpu.SemaphoreType.DMA((states,)), pltpu.SemaphoreType.DMA],
        compiler_params=pltpu.CompilerParams(collective_id=1, has_side_effects=True, vmem_limit_bytes=56 * 2**20),
    )(feats, lists, counts, *ws)


def rest_kernel(states, all_ref, early, lims, *refs):
    weights, out = refs[:6], refs[6]
    net = Net(weights, refs[7:])
    net.clear()
    net.prepare()

    def fetch(i):
        s = lax.rem(i, 2)
        return pltpu.make_async_copy(all_ref.at[i], net.xbuf.at[s], net.xsem.at[s])

    def within(lim):
        return (jnp.min(lim[0]) > 2.0**-80) & (jnp.max(lim[1]) < 2.0**100)

    out[:, 0:EARLY] = early[...]
    net.run(EARLY, states - EARLY, lambda s: net.attention(s, False), fetch, out, 0)

    @pl.when(jnp.logical_not(within(lims) & within(net.lim)))
    def _():
        net.run(0, states, lambda s: net.attention(s, True), fetch, out, 0)


def rest(every, early, lims, ws, states):
    return pl.pallas_call(
        functools.partial(rest_kernel, states),
        out_shape=jax.ShapeDtypeStruct((2, states, 128), f32),
        in_specs=[ANY] + [V] * 8,
        out_specs=V,
        scratch_shapes=scratch(),
        compiler_params=pltpu.CompilerParams(vmem_limit_bytes=56 * 2**20),
    )(every, early, lims, *ws)


def solve_kernel(states, walks, *refs):
    parts, pot, energy, mean, mat, rows, ssem, rsem, wssem, wrsem = refs
    me, mw = lax.axis_index("state"), lax.axis_index("walk")
    barrier = pltpu.get_barrier_semaphore()
    for d in range(1, states):
        pl.semaphore_signal(barrier, inc=1, device_id=(lax.rem(me + d, states), mw), device_id_type=MESH)
    for d in range(1, walks):
        pl.semaphore_signal(barrier, inc=1, device_id=(me, lax.rem(mw + d, walks)), device_id_type=MESH)

    lane = lax.broadcasted_iota(jnp.int32, (states, 128), 1)
    row_at = lax.broadcasted_iota(jnp.int32, (states, 128), 0)
    offset = functools.reduce(lambda a, p: jnp.where(row_at == p, OFFSETS[p], a), range(states), row_at)
    config = jnp.bitwise_xor(offset, me)

    def spread(t):
        value = jnp.sum(parts[t], axis=1, keepdims=True)
        return jnp.sum(jnp.where(lane == config + (1 - t) * states, value, 0.0), axis=0, keepdims=True)

    lane1 = lane[0:1]
    amp = spread(0)
    ham = spread(1)
    eye = jnp.where(lane1 == me + states, 1.0, 0.0)
    psi = jnp.where(lane1 < states, 0.0, eye + 0.9 / states * jnp.tanh(amp))
    mat[pl.ds(me, 1), :] = ham + jnp.where(lane1 < 2 * states, psi, 0.0)
    pl.semaphore_wait(barrier, states - 1 + walks - 1)

    def send(d):
        return pltpu.make_async_remote_copy(
            src_ref=mat.at[pl.ds(me, 1)], dst_ref=mat.at[pl.ds(me, 1)], send_sem=ssem.at[d], recv_sem=rsem.at[d],
            device_id=(lax.rem(me + d, states), mw), device_id_type=MESH,
        )

    for d in range(1, states):
        send(d).start()
    for d in range(1, states):
        came = lax.rem(me + states - d, states)
        pltpu.make_async_remote_copy(
            src_ref=mat.at[pl.ds(me, 1)], dst_ref=mat.at[pl.ds(came, 1)], send_sem=ssem.at[d], recv_sem=rsem.at[d],
            device_id=(lax.rem(me + d, states), mw), device_id_type=MESH,
        ).wait_recv()
    m = mat[...]
    for k in range(states):
        pivot_row = m[k : k + 1, :]
        scaled = pivot_row / pivot_row[:, states + k : states + k + 1]
        column = m[:, states + k : states + k + 1]
        m = jnp.where(row_at == k, scaled, m - column * scaled)
    mine = jnp.sum(jnp.where(row_at == me, m, 0.0), axis=0, keepdims=True)
    mine = jnp.where(lane1 == me, mine + pot[...], mine)
    energy[...] = mine[:, :states]
    rows[pl.ds(mw, 1), :] = mine

    def send_row(d):
        return pltpu.make_async_remote_copy(
            src_ref=rows.at[pl.ds(mw, 1)], dst_ref=rows.at[pl.ds(mw, 1)], send_sem=wssem.at[d], recv_sem=wrsem.at[d],
            device_id=(me, lax.rem(mw + d, walks)), device_id_type=MESH,
        )

    for d in range(1, walks):
        send_row(d).start()
    for d in range(1, walks):
        came = lax.rem(mw + walks - d, walks)
        pltpu.make_async_remote_copy(
            src_ref=rows.at[pl.ds(mw, 1)], dst_ref=rows.at[pl.ds(came, 1)], send_sem=wssem.at[d], recv_sem=wrsem.at[d],
            device_id=(me, lax.rem(mw + d, walks)), device_id_type=MESH,
        ).wait_recv()
    mean[...] = (jnp.sum(rows[...], axis=0, keepdims=True) * (1.0 / walks))[:, :states]
    for d in range(1, states):
        send(d).wait_send()
    for d in range(1, walks):
        send_row(d).wait_send()


def solve(parts, potential, states, walks):
    dma = pltpu.SemaphoreType.DMA
    return pl.pallas_call(
        functools.partial(solve_kernel, states, walks),
        out_shape=(jax.ShapeDtypeStruct((1, states), f32), jax.ShapeDtypeStruct((1, states), f32)),
        in_specs=[V, V],
        out_specs=(V, V),
        scratch_shapes=[
            pltpu.VMEM((states, 128), f32),
            pltpu.VMEM((walks, 128), f32),
            dma((states,)), dma((states,)), dma((walks,)), dma((walks,)),
        ],
        compiler_params=pltpu.CompilerParams(collective_id=0, has_side_effects=True),
    )(parts, potential)


def local(features, key_blocks, block_counts, potential, w_qkv, w_out, w_up, w_down, gains, readouts):
    states, walks = lax.axis_size("state"), lax.axis_size("walk")
    ws = (w_qkv[0], w_out[0], w_up[0], w_down[0], gains[0], readouts[0])
    every, early, lims = gather(features[0, 0], key_blocks[0, 0], block_counts[0], ws, states)
    parts = rest(every, early, lims, ws, states)
    energy, mean = solve(parts, potential, states, walks)
    return energy[:, :, None], mean


def solution(mesh):
    placed = (
        P("state", "walk", None, None),
        P("state", "walk", None, None),
        P("state", "walk", None),
        P("state", "walk"),
        P("state", None, None, None),
        P("state", None, None, None),
        P("state", None, None, None),
        P("state", None, None, None),
        P("state", None, None),
        P("state", None, None),
    )
    return jax.shard_map(
        local,
        mesh=mesh,
        in_specs=placed,
        out_specs=(P("state", None, "walk"), P("state", None)),
        check_vma=False,
    )
```

```python
import functools
import itertools

import jax
import jax.numpy as jnp
from jax import lax
from jax.experimental import pallas as pl
from jax.experimental.pallas import tpu as pltpu
from jax.sharding import PartitionSpec as P

D = 256
A = 512
B = 128
NB = 4
H = 8
SLOTS = 3
EXTRA = 16
COUNTS = 8
EARLY = 5
AHEAD = 8
OFFSETS = (0, 1, 4, 5, 12, 13, 2, 3, 6, 7, 14, 15, 8, 9, 10, 11)
DIRECT = (1, 2, 4, 6)
QS = 1.4426950408889634 / 32.0**0.5
bf = jnp.bfloat16
f32 = jnp.float32
MESH = pl.DeviceIdType.MESH
V = pl.BlockSpec(memory_space=pltpu.VMEM)
ANY = pl.BlockSpec(memory_space=pl.ANY)


def mm(a, b):
    return lax.dot_general(a, b, (((1,), (0,)), ((), ())), preferred_element_type=f32)


def rscale(h):
    return lax.rsqrt(jnp.sum(h * h, axis=0, keepdims=True) * (1.0 / D) + 1e-6)


def norm(h, g):
    r = rscale(h)
    parts = [((h[:, c : c + 128] * r[:, c : c + 128]) * g).astype(bf) for c in range(0, h.shape[1], 128)]
    return jnp.concatenate(parts, axis=1)


class Net:
    def __init__(self, weights, scratch):
        self.raw = weights
        self.wqkv, self.wo, self.wu, self.wd, self.gn, self.gr = scratch[:6]
        self.h, self.k, self.v, self.qx, self.a, self.lim = scratch[6:12]
        self.ivm, self.ism, self.isem, self.xbuf, self.xsem = scratch[12:]

    def clear(self):
        self.qx[...] = jnp.zeros(self.qx.shape, bf)
        self.v[...] = jnp.ones(self.v.shape, bf)
        self.lim[...] = jnp.ones(self.lim.shape, f32)

    def prepare(self):
        *mats, gains, readouts = self.raw

        def layer(l, _):
            for w, t in zip(mats, (self.wqkv, self.wo, self.wu, self.wd)):
                for r in range(0, w.shape[1], 256):
                    for c in range(0, w.shape[2], 256):
                        tile = w[l, r : r + 256, c : c + 256].T
                        t[l, c : c + 256, r : r + 256] = tile * bf(0.5) if t is self.wd else tile
            return 0

        lax.fori_loop(0, 2, layer, 0)

        def column(row):
            return jnp.broadcast_to(row, (128, D)).T

        for r in range(4):
            self.gn[r] = column(gains[r])
        last = gains[4] * (1.0 / A**0.5)
        for t in range(2):
            self.gr[t] = column(last * readouts[t : t + 1, :])

    def ints(self, s):
        self.ivm[...] = self.xbuf[s, D : D + EXTRA, 0:128].astype(f32).astype(jnp.int32)
        return pltpu.make_async_copy(self.ivm, self.ism.at[s], self.isem)

    def project(self, l, c, h):
        n = norm(h, self.gn[2 * l])
        q = (mm(self.wqkv[l, 0:256, :], n) * QS).astype(bf)
        k = mm(self.wqkv[l, 256:512, :], n).astype(bf).T
        v = mm(self.wqkv[l, 512:768, :], n).astype(bf)
        for head in range(H):
            row, lane = (head % 4) * 32, (head % 2) * 128
            for b in range(2):
                self.qx[2 * c + b, head // 2, row : row + 32, lane : lane + 128] = q[
                    head * 32 : head * 32 + 32, b * 128 : b * 128 + 128
                ]
        for b in range(2):
            self.k[2 * c + b] = k[b * 128 : b * 128 + 128, :]
            for p in range(4):
                self.v[2 * c + b, p, 0:64, :] = v[p * 64 : p * 64 + 64, b * 128 : b * 128 + 128]

    def scores(self, b, kbs, p):
        half = p // 2 * 128
        return [mm(self.k[kb, :, half : half + 128], self.qx[b, p]) for kb in kbs]

    def mix(self, ss, kbs, p, keep, safe):
        if safe:
            top = functools.reduce(jnp.maximum, [jnp.max(s, axis=0, keepdims=True) for s in ss])
            ss = [s - top for s in ss]
        ps = [jnp.exp2(s).astype(bf) for s in ss]
        if keep is not None:
            ps = [jnp.where(ok, q, jnp.zeros_like(q)) if s else q for s, (ok, q) in enumerate(zip(keep, ps))]
        vs = [self.v[kb, p] for kb in kbs]
        return mm(jnp.concatenate(vs, axis=1), jnp.concatenate(ps, axis=0))

    def emit(self, o, b, p):
        den = o[64:72, :]
        inv = 1.0 / den[0:1]
        lanes = pl.ds(b * 128 if isinstance(b, int) else pl.multiple_of(b * 128, 128), 128)
        self.a[p * 64 : p * 64 + 32, lanes] = (o[0:32, :128] * inv[:, :128]).astype(bf)
        self.a[p * 64 + 32 : p * 64 + 64, lanes] = (o[32:64, 128:] * inv[:, 128:]).astype(bf)
        return den

    def attend(self, items, safe):
        units = [(b, kbs, keep, p) for b, kbs, keep in items for p in range(4)]
        ss = [self.scores(b, kbs, p) for b, kbs, _, p in units[:AHEAD]]
        dens = []
        for n, (b, kbs, keep, p) in enumerate(units):
            if n + AHEAD < len(units):
                later = units[n + AHEAD]
                ss.append(self.scores(later[0], later[1], later[3]))
            dens.append(self.emit(self.mix(ss[n], kbs, p, keep, safe), b, p))
        if not safe:
            self.lim[0] = jnp.minimum(self.lim[0], functools.reduce(jnp.minimum, dens))
            self.lim[1] = jnp.maximum(self.lim[1], functools.reduce(jnp.maximum, dens))

    def attention_masked(self, s):
        items = []
        for b in range(NB):
            count = self.ism[s, COUNTS, b]
            kbs = [jnp.clip(self.ism[s, t, b], 0, NB - 1) for t in range(SLOTS)]
            items.append((b, kbs, [count > t for t in range(SLOTS)]))
        self.attend(items, False)

    def attention(self, s, safe):
        count = [self.ism[s, COUNTS, b] for b in range(1, NB)]
        block = [jnp.int32(b) for b in range(1, NB)]
        for x, y in ((0, 1), (1, 2), (0, 1)):
            swap = count[y] > count[x]
            for seq in (count, block):
                seq[x], seq[y] = jnp.where(swap, seq[y], seq[x]), jnp.where(swap, seq[x], seq[y])
        for case in itertools.combinations_with_replacement(range(SLOTS, 0, -1), NB - 1):

            @pl.when((count[0] == case[0]) & (count[1] == case[1]) & (count[2] == case[2]))
            def _(case=case):
                todo = zip([0, *block], (SLOTS, *case))
                self.attend([(b, [self.ism[s, t, b] for t in range(c)], None) for b, c in todo], safe)

    def feed(self, l, then):
        h = self.h[...] + mm(self.wo[l], self.a[...])
        u = mm(self.wu[l], norm(h, self.gn[2 * l + 1]))
        z = u * (0.7978845608028654 + 0.035677408136300125 * (u * u))
        h = h + mm(self.wd[l], (u + u * jnp.tanh(z)).astype(bf))
        for c in range(2):
            then(c, h[:, c * 256 : c * 256 + 256])

    def final(self, h, sums):
        r = rscale(h)
        out = []
        for t in range(2):
            g, acc = self.gr[t], sums[t]
            for c in range(0, h.shape[1], 128):
                acc = acc + jnp.sum(h[:, c : c + 128] * g, axis=0, keepdims=True) * r[:, c : c + 128]
            out.append(acc)
        return out

    def run(self, first, count, attention, fetch, out, at, between=None):
        def begin(s):
            return [self.xbuf[s, 0:D, c * 256 : c * 256 + 256].astype(f32) for c in range(2)]

        s0 = first % 2
        fetch(first).start()
        fetch(first).wait()
        lists = self.ints(s0)
        lists.start()
        for c, h in enumerate(begin(s0)):
            self.h[:, c * 256 : c * 256 + 256] = h
            self.project(0, c, h)
        lists.wait()

        def config(i, _):
            s = lax.rem(i, 2)
            if between is not None:
                between(i)

            @pl.when(i + 1 < first + count)
            def _():
                fetch(i + 1).start()

            def layer(l, _):
                attention(s)

                @pl.when(l == 0)
                def _():
                    @pl.when(i + 1 < first + count)
                    def _():
                        fetch(i + 1).wait()
                        self.ints(1 - s).start()

                    def then(c, h):
                        self.h[:, c * 256 : c * 256 + 256] = h
                        self.project(1, c, h)

                    self.feed(0, then)

                @pl.when(l == 1)
                def _():
                    sums = [[0.0, 0.0]]
                    later = begin(1 - s)
                    for c in range(2):
                        self.project(0, c, later[c])
                    self.feed(1, lambda c, h: sums.append(self.final(h, sums[-1])))
                    for c in range(2):
                        self.h[:, c * 256 : c * 256 + 256] = later[c]
                    for t in range(2):
                        out[t, pl.ds(i - at, 1)] = sums[-1][t]

                    @pl.when(i + 1 < first + count)
                    def _():
                        pltpu.make_async_copy(self.ivm, self.ism.at[1 - s], self.isem).wait()

                return 0

            lax.fori_loop(0, 2, layer, 0)
            return 0

        lax.fori_loop(first, first + count, config, 0)


def scratch():
    return [
        pltpu.VMEM((2, 3 * D, D), bf),
        pltpu.VMEM((2, D, D), bf),
        pltpu.VMEM((2, 2 * D, D), bf),
        pltpu.VMEM((2, D, 2 * D), bf),
        pltpu.VMEM((4, D, 128), f32),
        pltpu.VMEM((2, D, 128), f32),
        pltpu.VMEM((D, A), f32),
        pltpu.VMEM((NB, B, D), bf),
        pltpu.VMEM((NB, 4, 80, B), bf),
        pltpu.VMEM((NB, 4, B, 2 * B), bf),
        pltpu.VMEM((D, A), bf),
        pltpu.VMEM((2, 8, 2 * B), f32),
        pltpu.VMEM((EXTRA, 128), jnp.int32),
        pltpu.SMEM((2, EXTRA, 128), jnp.int32),
        pltpu.SemaphoreType.DMA,
        pltpu.VMEM((2, D + EXTRA, A), bf),
        pltpu.SemaphoreType.DMA((2,)),
    ]


def flip(me, k):
    out = 0
    for bit in (1, 2, 4, 8):
        mine = lax.rem(lax.div(me, bit), 2)
        out = out + bit * ((1 - mine) if k & bit else mine)
    return out


def gather_kernel(states, feats, lists, counts, *refs):
    weights, (all_ref, out, lims) = refs[:6], refs[6:9]
    net = Net(weights, refs[9:26])
    x_ref, ssem, rsem, csem = refs[26:]
    me, mw = lax.axis_index("state"), lax.axis_index("walk")
    barrier = pltpu.get_barrier_semaphore()
    for k in DIRECT:
        pl.semaphore_signal(barrier, inc=1, device_id=(flip(me, OFFSETS[k]), mw), device_id_type=MESH)
    x_ref[0:D, :] = feats[...].T
    net.ivm[...] = jnp.zeros(net.ivm.shape, jnp.int32)
    for t in range(SLOTS):
        net.ivm[t : t + 1, 0:NB] = lists[t]
    net.ivm[COUNTS : COUNTS + 1, 0:NB] = counts[...]
    x_ref[D : D + EXTRA, :] = jnp.zeros((EXTRA, A), bf)
    x_ref[D : D + EXTRA, 0:128] = net.ivm[...].astype(f32).astype(bf)
    own = pltpu.make_async_copy(x_ref, all_ref.at[0], csem)
    own.start()
    pl.semaphore_wait(barrier, len(DIRECT))

    near = lax.rem(lax.rem(lax.div(me, 4), 2) + lax.rem(me, 2), 2) == 0
    onward = jnp.where(near, flip(me, 4), flip(me, 12))

    def push(src, k, device):
        return pltpu.make_async_remote_copy(
            src_ref=src, dst_ref=all_ref.at[k], send_sem=ssem.at[k], recv_sem=rsem.at[k],
            device_id=(device, mw), device_id_type=MESH,
        )

    def copy(k):
        if k in DIRECT:
            return push(x_ref, k, flip(me, OFFSETS[k]))
        if k % 2:
            return push(all_ref.at[k - 1], k, flip(me, 1))
        if k in (8, 10):
            return push(all_ref.at[6], k, flip(me, 4 if k == 8 else 12))
        one, other = (2, 4) if k == 12 else (8, 10)
        return push(all_ref.at[jnp.where(near, other, one)], k, onward)

    def landed(*slots):
        for k in slots:
            copy(k).wait_recv()
            if k % 2 == 0:
                copy(k + 1).start()

    for k in DIRECT:
        copy(k).start()
    net.clear()
    net.prepare()
    own.wait()

    def fetch(i):
        s = lax.rem(i, 2)
        return pltpu.make_async_copy(all_ref.at[i], net.xbuf.at[s], net.xsem.at[s])

    def between(i):
        @pl.when(i == 0)
        def _():
            landed(1)

        @pl.when(i == 1)
        def _():
            landed(2, 4)
            copy(12).start()

        @pl.when(i == 2)
        def _():
            landed(6)
            copy(8).start()
            copy(10).start()
            copy(3).wait_recv()

        @pl.when(i == 3)
        def _():
            landed(8, 10)
            copy(14).start()
            landed(12)

        @pl.when(i == 4)
        def _():
            landed(14)

    net.run(0, EARLY, net.attention_masked, fetch, out, 0, between)
    for k in range(5, states, 2):
        copy(k).wait_recv()
    for k in range(1, states):
        copy(k).wait_send()
    lims[...] = net.lim[...]


def gather(feats, lists, counts, ws, states):
    return pl.pallas_call(
        functools.partial(gather_kernel, states),
        out_shape=(
            jax.ShapeDtypeStruct((states, D + EXTRA, A), bf),
            jax.ShapeDtypeStruct((2, EARLY, 128), f32),
            jax.ShapeDtypeStruct((2, 8, 2 * B), f32),
        ),
        in_specs=[V] * 9,
        out_specs=(ANY, V, V),
        scratch_shapes=scratch()
        + [pltpu.VMEM((D + EXTRA, A), bf)]
        + [pltpu.SemaphoreType.DMA((states,)), pltpu.SemaphoreType.DMA((states,)), pltpu.SemaphoreType.DMA],
        compiler_params=pltpu.CompilerParams(collective_id=1, has_side_effects=True, vmem_limit_bytes=56 * 2**20),
    )(feats, lists, counts, *ws)


def rest_kernel(states, all_ref, early, lims, *refs):
    weights, out = refs[:6], refs[6]
    net = Net(weights, refs[7:])
    net.clear()
    net.prepare()

    def fetch(i):
        s = lax.rem(i, 2)
        return pltpu.make_async_copy(all_ref.at[i], net.xbuf.at[s], net.xsem.at[s])

    def within(lim):
        return (jnp.min(lim[0]) > 2.0**-80) & (jnp.max(lim[1]) < 2.0**100)

    out[:, 0:EARLY] = early[...]
    net.run(EARLY, states - EARLY, lambda s: net.attention(s, False), fetch, out, 0)

    @pl.when(jnp.logical_not(within(lims) & within(net.lim)))
    def _():
        net.run(0, states, lambda s: net.attention(s, True), fetch, out, 0)


def rest(every, early, lims, ws, states):
    return pl.pallas_call(
        functools.partial(rest_kernel, states),
        out_shape=jax.ShapeDtypeStruct((2, states, 128), f32),
        in_specs=[ANY] + [V] * 8,
        out_specs=V,
        scratch_shapes=scratch(),
        compiler_params=pltpu.CompilerParams(vmem_limit_bytes=56 * 2**20),
    )(every, early, lims, *ws)


def solve_kernel(states, walks, *refs):
    parts, pot, energy, mean, mat, rows, ssem, rsem, wssem, wrsem = refs
    me, mw = lax.axis_index("state"), lax.axis_index("walk")
    barrier = pltpu.get_barrier_semaphore()
    for d in range(1, states):
        pl.semaphore_signal(barrier, inc=1, device_id=(lax.rem(me + d, states), mw), device_id_type=MESH)
    for d in range(1, walks):
        pl.semaphore_signal(barrier, inc=1, device_id=(me, lax.rem(mw + d, walks)), device_id_type=MESH)

    lane = lax.broadcasted_iota(jnp.int32, (states, 128), 1)
    row_at = lax.broadcasted_iota(jnp.int32, (states, 128), 0)
    offset = functools.reduce(lambda a, p: jnp.where(row_at == p, OFFSETS[p], a), range(states), row_at)
    config = jnp.bitwise_xor(offset, me)

    def spread(t):
        value = jnp.sum(parts[t], axis=1, keepdims=True)
        return jnp.sum(jnp.where(lane == config + (1 - t) * states, value, 0.0), axis=0, keepdims=True)

    lane1 = lane[0:1]
    amp = spread(0)
    ham = spread(1)
    eye = jnp.where(lane1 == me + states, 1.0, 0.0)
    psi = jnp.where(lane1 < states, 0.0, eye + 0.9 / states * jnp.tanh(amp))
    mat[pl.ds(me, 1), :] = ham + jnp.where(lane1 < 2 * states, psi, 0.0)
    pl.semaphore_wait(barrier, states - 1 + walks - 1)

    def send(d):
        return pltpu.make_async_remote_copy(
            src_ref=mat.at[pl.ds(me, 1)], dst_ref=mat.at[pl.ds(me, 1)], send_sem=ssem.at[d], recv_sem=rsem.at[d],
            device_id=(lax.rem(me + d, states), mw), device_id_type=MESH,
        )

    for d in range(1, states):
        send(d).start()
    for d in range(1, states):
        came = lax.rem(me + states - d, states)
        pltpu.make_async_remote_copy(
            src_ref=mat.at[pl.ds(me, 1)], dst_ref=mat.at[pl.ds(came, 1)], send_sem=ssem.at[d], recv_sem=rsem.at[d],
            device_id=(lax.rem(me + d, states), mw), device_id_type=MESH,
        ).wait_recv()
    m = mat[...]
    for k in range(states):
        pivot_row = m[k : k + 1, :]
        scaled = pivot_row / pivot_row[:, states + k : states + k + 1]
        column = m[:, states + k : states + k + 1]
        m = jnp.where(row_at == k, scaled, m - column * scaled)
    mine = jnp.sum(jnp.where(row_at == me, m, 0.0), axis=0, keepdims=True)
    mine = jnp.where(lane1 == me, mine + pot[...], mine)
    energy[...] = mine
    rows[pl.ds(mw, 1), :] = mine

    def send_row(d):
        return pltpu.make_async_remote_copy(
            src_ref=rows.at[pl.ds(mw, 1)], dst_ref=rows.at[pl.ds(mw, 1)], send_sem=wssem.at[d], recv_sem=wrsem.at[d],
            device_id=(me, lax.rem(mw + d, walks)), device_id_type=MESH,
        )

    for d in range(1, walks):
        send_row(d).start()
    for d in range(1, walks):
        came = lax.rem(mw + walks - d, walks)
        pltpu.make_async_remote_copy(
            src_ref=rows.at[pl.ds(mw, 1)], dst_ref=rows.at[pl.ds(came, 1)], send_sem=wssem.at[d], recv_sem=wrsem.at[d],
            device_id=(me, lax.rem(mw + d, walks)), device_id_type=MESH,
        ).wait_recv()
    mean[...] = jnp.sum(rows[...], axis=0, keepdims=True) * (1.0 / walks)
    for d in range(1, states):
        send(d).wait_send()
    for d in range(1, walks):
        send_row(d).wait_send()


def solve(parts, potential, states, walks):
    dma = pltpu.SemaphoreType.DMA
    return pl.pallas_call(
        functools.partial(solve_kernel, states, walks),
        out_shape=(jax.ShapeDtypeStruct((1, 128), f32), jax.ShapeDtypeStruct((1, 128), f32)),
        in_specs=[V, V],
        out_specs=(V, V),
        scratch_shapes=[
            pltpu.VMEM((states, 128), f32),
            pltpu.VMEM((walks, 128), f32),
            dma((states,)), dma((states,)), dma((walks,)), dma((walks,)),
        ],
        compiler_params=pltpu.CompilerParams(collective_id=0, has_side_effects=True),
    )(parts, potential)


def trim_kernel(energy, mean, energy_out, mean_out):
    n = energy_out.shape[1]
    energy_out[...] = energy[:, :n]
    mean_out[...] = mean[:, :n]


def trim(energy, mean, states):
    shape = jax.ShapeDtypeStruct((1, states), f32)
    return pl.pallas_call(trim_kernel, out_shape=(shape, shape), in_specs=[V, V], out_specs=(V, V))(energy, mean)


def local(features, key_blocks, block_counts, potential, w_qkv, w_out, w_up, w_down, gains, readouts):
    states, walks = lax.axis_size("state"), lax.axis_size("walk")
    ws = (w_qkv[0], w_out[0], w_up[0], w_down[0], gains.transpose(1, 0, 2), readouts[0])
    every, early, lims = gather(features[0, 0], key_blocks[0].transpose(2, 0, 1), block_counts[0], ws, states)
    parts = rest(every, early, lims, ws, states)
    energy, mean = trim(*solve(parts, potential, states, walks), states)
    return energy[:, :, None], mean


def solution(mesh):
    placed = (
        P("state", "walk", None, None),
        P("state", "walk", None, None),
        P("state", "walk", None),
        P("state", "walk"),
        P("state", None, None, None),
        P("state", None, None, None),
        P("state", None, None, None),
        P("state", None, None, None),
        P("state", None, None),
        P("state", None, None),
    )
    return jax.shard_map(
        local,
        mesh=mesh,
        in_specs=placed,
        out_specs=(P("state", None, "walk"), P("state", None)),
        check_vma=False,
    )
```

```python
import functools
import itertools

import jax
import jax.numpy as jnp
from jax import lax
from jax.experimental import pallas as pl
from jax.experimental.pallas import tpu as pltpu
from jax.sharding import PartitionSpec as P

D = 256
A = 512
B = 128
NB = 4
H = 8
SLOTS = 3
EXTRA = 16
COUNTS = 8
EARLY = 5
AHEAD = 8
OFFSETS = (0, 1, 4, 5, 12, 13, 2, 3, 6, 7, 14, 15, 8, 9, 10, 11)
DIRECT = (1, 2, 4, 6)
QS = 1.4426950408889634 / 32.0**0.5
bf = jnp.bfloat16
f32 = jnp.float32
MESH = pl.DeviceIdType.MESH
V = pl.BlockSpec(memory_space=pltpu.VMEM)
ANY = pl.BlockSpec(memory_space=pl.ANY)


def mm(a, b):
    return lax.dot_general(a, b, (((1,), (0,)), ((), ())), preferred_element_type=f32)


def rscale(h):
    return lax.rsqrt(jnp.sum(h * h, axis=0, keepdims=True) * (1.0 / D) + 1e-6)


def norm(h, g):
    r = rscale(h)
    parts = [((h[:, c : c + 128] * r[:, c : c + 128]) * g).astype(bf) for c in range(0, h.shape[1], 128)]
    return jnp.concatenate(parts, axis=1)


class Net:
    def __init__(self, weights, scratch):
        self.raw = weights
        self.wqkv, self.wo, self.wu, self.wd, self.gn, self.gr = scratch[:6]
        self.h, self.k, self.v, self.qx, self.a, self.lim = scratch[6:12]
        self.ivm, self.ism, self.isem, self.xbuf, self.xsem = scratch[12:]

    def clear(self):
        self.qx[...] = jnp.zeros(self.qx.shape, bf)
        self.v[...] = jnp.ones(self.v.shape, bf)
        self.lim[...] = jnp.ones(self.lim.shape, f32)

    def prepare(self):
        *mats, gains, readouts = self.raw

        def layer(l, _):
            for w, t in zip(mats, (self.wqkv, self.wo, self.wu, self.wd)):
                for r in range(0, w.shape[1], 256):
                    for c in range(0, w.shape[2], 256):
                        tile = w[l, r : r + 256, c : c + 256].T
                        t[l, c : c + 256, r : r + 256] = tile * bf(0.5) if t is self.wd else tile
            return 0

        lax.fori_loop(0, 2, layer, 0)

        def column(row):
            return jnp.broadcast_to(row, (128, D)).T

        for r in range(4):
            self.gn[r] = column(gains[r])
        last = gains[4] * (1.0 / A**0.5)
        for t in range(2):
            self.gr[t] = column(last * readouts[t : t + 1, :])

    def ints(self, s):
        self.ivm[...] = self.xbuf[s, D : D + EXTRA, 0:128].astype(f32).astype(jnp.int32)
        return pltpu.make_async_copy(self.ivm, self.ism.at[s], self.isem)

    def project(self, l, c, h):
        n = norm(h, self.gn[2 * l])
        k = mm(self.wqkv[l, 256:512, :], n).astype(bf).T
        q = (mm(self.wqkv[l, 0:256, :], n) * QS).astype(bf)
        v = mm(self.wqkv[l, 512:768, :], n).astype(bf)
        for head in range(H):
            row, lane = (head % 4) * 32, (head % 2) * 128
            for b in range(2):
                self.qx[2 * c + b, head // 2, row : row + 32, lane : lane + 128] = q[
                    head * 32 : head * 32 + 32, b * 128 : b * 128 + 128
                ]
        for b in range(2):
            self.k[2 * c + b] = k[b * 128 : b * 128 + 128, :]
            for p in range(4):
                self.v[2 * c + b, p, 0:64, :] = v[p * 64 : p * 64 + 64, b * 128 : b * 128 + 128]

    def scores(self, b, kbs, p):
        half = p // 2 * 128
        return [mm(self.k[kb, :, half : half + 128], self.qx[b, p]) for kb in kbs]

    def mix(self, ss, kbs, p, keep, safe):
        if safe:
            top = functools.reduce(jnp.maximum, [jnp.max(s, axis=0, keepdims=True) for s in ss])
            ss = [s - top for s in ss]
        ps = [jnp.exp2(s).astype(bf) for s in ss]
        if keep is not None:
            ps = [jnp.where(ok, q, jnp.zeros_like(q)) if s else q for s, (ok, q) in enumerate(zip(keep, ps))]
        vs = [self.v[kb, p] for kb in kbs]
        return mm(jnp.concatenate(vs, axis=1), jnp.concatenate(ps, axis=0))

    def emit(self, o, b, p):
        den = o[64:72, :]
        inv = 1.0 / den[0:1]
        lanes = pl.ds(b * 128 if isinstance(b, int) else pl.multiple_of(b * 128, 128), 128)
        self.a[p * 64 : p * 64 + 32, lanes] = (o[0:32, :128] * inv[:, :128]).astype(bf)
        self.a[p * 64 + 32 : p * 64 + 64, lanes] = (o[32:64, 128:] * inv[:, 128:]).astype(bf)
        return den

    def attend(self, items, safe):
        units = [(b, kbs, keep, p) for b, kbs, keep in items for p in range(4)]
        ss = [self.scores(b, kbs, p) for b, kbs, _, p in units[:AHEAD]]
        dens = []
        for n, (b, kbs, keep, p) in enumerate(units):
            if n + AHEAD < len(units):
                later = units[n + AHEAD]
                ss.append(self.scores(later[0], later[1], later[3]))
            dens.append(self.emit(self.mix(ss[n], kbs, p, keep, safe), b, p))
        if not safe:
            self.lim[0] = jnp.minimum(self.lim[0], functools.reduce(jnp.minimum, dens))
            self.lim[1] = jnp.maximum(self.lim[1], functools.reduce(jnp.maximum, dens))

    def attention_masked(self, s):
        items = []
        for b in range(NB):
            count = self.ism[s, COUNTS, b]
            kbs = [jnp.clip(self.ism[s, t, b], 0, NB - 1) for t in range(SLOTS)]
            items.append((b, kbs, [count > t for t in range(SLOTS)]))
        self.attend(items, False)

    def attention(self, s, safe):
        count = [self.ism[s, COUNTS, b] for b in range(1, NB)]
        block = [jnp.int32(b) for b in range(1, NB)]
        for x, y in ((0, 1), (1, 2), (0, 1)):
            swap = count[y] > count[x]
            for seq in (count, block):
                seq[x], seq[y] = jnp.where(swap, seq[y], seq[x]), jnp.where(swap, seq[x], seq[y])
        for case in itertools.combinations_with_replacement(range(SLOTS, 0, -1), NB - 1):

            @pl.when((count[0] == case[0]) & (count[1] == case[1]) & (count[2] == case[2]))
            def _(case=case):
                todo = zip([0, *block], (SLOTS, *case))
                self.attend([(b, [self.ism[s, t, b] for t in range(c)], None) for b, c in todo], safe)

    def feed(self, l, then, fill=(lambda: None, lambda: None)):
        h = self.h[...] + mm(self.wo[l], self.a[...])
        fill[0]()
        u = mm(self.wu[l], norm(h, self.gn[2 * l + 1]))
        fill[1]()
        z = u * (0.7978845608028654 + 0.035677408136300125 * (u * u))
        h = h + mm(self.wd[l], (u + u * jnp.tanh(z)).astype(bf))
        for c in range(2):
            then(c, h[:, c * 256 : c * 256 + 256])

    def final(self, h, sums):
        r = rscale(h)
        out = []
        for t in range(2):
            g, acc = self.gr[t], sums[t]
            for c in range(0, h.shape[1], 128):
                acc = acc + jnp.sum(h[:, c : c + 128] * g, axis=0, keepdims=True) * r[:, c : c + 128]
            out.append(acc)
        return out

    def run(self, first, count, attention, fetch, out, at, between=None):
        def begin(s):
            return [self.xbuf[s, 0:D, c * 256 : c * 256 + 256].astype(f32) for c in range(2)]

        s0 = first % 2
        fetch(first).start()
        fetch(first).wait()
        lists = self.ints(s0)
        lists.start()
        for c, h in enumerate(begin(s0)):
            self.h[:, c * 256 : c * 256 + 256] = h
            self.project(0, c, h)
        lists.wait()

        def config(i, _):
            s = lax.rem(i, 2)
            if between is not None:
                between(i)

            @pl.when(i + 1 < first + count)
            def _():
                fetch(i + 1).start()

            def layer(l, _):
                attention(s)

                @pl.when(l == 0)
                def _():
                    @pl.when(i + 1 < first + count)
                    def _():
                        fetch(i + 1).wait()
                        self.ints(1 - s).start()

                    def then(c, h):
                        self.h[:, c * 256 : c * 256 + 256] = h
                        self.project(1, c, h)

                    self.feed(0, then)

                @pl.when(l == 1)
                def _():
                    sums = [[0.0, 0.0]]
                    later = begin(1 - s)
                    done = []
                    self.feed(1, lambda c, h: done.append(h), [functools.partial(self.project, 0, c, later[c]) for c in range(2)])
                    for h in done:
                        sums.append(self.final(h, sums[-1]))
                    for c in range(2):
                        self.h[:, c * 256 : c * 256 + 256] = later[c]
                    for t in range(2):
                        out[t, pl.ds(i - at, 1)] = sums[-1][t]

                    @pl.when(i + 1 < first + count)
                    def _():
                        pltpu.make_async_copy(self.ivm, self.ism.at[1 - s], self.isem).wait()

                return 0

            lax.fori_loop(0, 2, layer, 0)
            return 0

        lax.fori_loop(first, first + count, config, 0)


def scratch():
    return [
        pltpu.VMEM((2, 3 * D, D), bf),
        pltpu.VMEM((2, D, D), bf),
        pltpu.VMEM((2, 2 * D, D), bf),
        pltpu.VMEM((2, D, 2 * D), bf),
        pltpu.VMEM((4, D, 128), f32),
        pltpu.VMEM((2, D, 128), f32),
        pltpu.VMEM((D, A), f32),
        pltpu.VMEM((NB, B, D), bf),
        pltpu.VMEM((NB, 4, 80, B), bf),
        pltpu.VMEM((NB, 4, B, 2 * B), bf),
        pltpu.VMEM((D, A), bf),
        pltpu.VMEM((2, 8, 2 * B), f32),
        pltpu.VMEM((EXTRA, 128), jnp.int32),
        pltpu.SMEM((2, EXTRA, 128), jnp.int32),
        pltpu.SemaphoreType.DMA,
        pltpu.VMEM((2, D + EXTRA, A), bf),
        pltpu.SemaphoreType.DMA((2,)),
    ]


def flip(me, k):
    out = 0
    for bit in (1, 2, 4, 8):
        mine = lax.rem(lax.div(me, bit), 2)
        out = out + bit * ((1 - mine) if k & bit else mine)
    return out


def gather_kernel(states, feats, lists, counts, *refs):
    weights, (all_ref, out, lims) = refs[:6], refs[6:9]
    net = Net(weights, refs[9:26])
    x_ref, ssem, rsem, csem = refs[26:]
    me, mw = lax.axis_index("state"), lax.axis_index("walk")
    barrier = pltpu.get_barrier_semaphore()
    for k in DIRECT:
        pl.semaphore_signal(barrier, inc=1, device_id=(flip(me, OFFSETS[k]), mw), device_id_type=MESH)
    x_ref[0:D, :] = feats[...].T
    net.ivm[...] = jnp.zeros(net.ivm.shape, jnp.int32)
    for t in range(SLOTS):
        net.ivm[t : t + 1, 0:NB] = lists[t]
    net.ivm[COUNTS : COUNTS + 1, 0:NB] = counts[...]
    x_ref[D : D + EXTRA, :] = jnp.zeros((EXTRA, A), bf)
    x_ref[D : D + EXTRA, 0:128] = net.ivm[...].astype(f32).astype(bf)
    own = pltpu.make_async_copy(x_ref, all_ref.at[0], csem)
    own.start()
    pl.semaphore_wait(barrier, len(DIRECT))

    near = lax.rem(lax.rem(lax.div(me, 4), 2) + lax.rem(me, 2), 2) == 0
    onward = jnp.where(near, flip(me, 4), flip(me, 12))

    def push(src, k, device):
        return pltpu.make_async_remote_copy(
            src_ref=src, dst_ref=all_ref.at[k], send_sem=ssem.at[k], recv_sem=rsem.at[k],
            device_id=(device, mw), device_id_type=MESH,
        )

    def copy(k):
        if k in DIRECT:
            return push(x_ref, k, flip(me, OFFSETS[k]))
        if k % 2:
            return push(all_ref.at[k - 1], k, flip(me, 1))
        if k in (8, 10):
            return push(all_ref.at[6], k, flip(me, 4 if k == 8 else 12))
        one, other = (2, 4) if k == 12 else (8, 10)
        return push(all_ref.at[jnp.where(near, other, one)], k, onward)

    def landed(*slots):
        for k in slots:
            copy(k).wait_recv()
            if k % 2 == 0:
                copy(k + 1).start()

    for k in DIRECT:
        copy(k).start()
    net.clear()
    net.prepare()
    own.wait()

    def fetch(i):
        s = lax.rem(i, 2)
        return pltpu.make_async_copy(all_ref.at[i], net.xbuf.at[s], net.xsem.at[s])

    def between(i):
        @pl.when(i == 0)
        def _():
            landed(1)

        @pl.when(i == 1)
        def _():
            landed(2, 4)
            copy(12).start()

        @pl.when(i == 2)
        def _():
            landed(6)
            copy(8).start()
            copy(10).start()
            copy(3).wait_recv()

        @pl.when(i == 3)
        def _():
            landed(8, 10)
            copy(14).start()
            landed(12)

        @pl.when(i == 4)
        def _():
            landed(14)

    net.run(0, EARLY, net.attention_masked, fetch, out, 0, between)
    for k in range(5, states, 2):
        copy(k).wait_recv()
    for k in range(1, states):
        copy(k).wait_send()
    lims[...] = net.lim[...]


def gather(feats, lists, counts, ws, states):
    return pl.pallas_call(
        functools.partial(gather_kernel, states),
        out_shape=(
            jax.ShapeDtypeStruct((states, D + EXTRA, A), bf),
            jax.ShapeDtypeStruct((2, EARLY, 128), f32),
            jax.ShapeDtypeStruct((2, 8, 2 * B), f32),
        ),
        in_specs=[V] * 9,
        out_specs=(ANY, V, V),
        scratch_shapes=scratch()
        + [pltpu.VMEM((D + EXTRA, A), bf)]
        + [pltpu.SemaphoreType.DMA((states,)), pltpu.SemaphoreType.DMA((states,)), pltpu.SemaphoreType.DMA],
        compiler_params=pltpu.CompilerParams(collective_id=1, has_side_effects=True, vmem_limit_bytes=56 * 2**20),
    )(feats, lists, counts, *ws)


def rest_kernel(states, all_ref, early, lims, *refs):
    weights, out = refs[:6], refs[6]
    net = Net(weights, refs[7:])
    net.clear()
    net.prepare()

    def fetch(i):
        s = lax.rem(i, 2)
        return pltpu.make_async_copy(all_ref.at[i], net.xbuf.at[s], net.xsem.at[s])

    def within(lim):
        return (jnp.min(lim[0]) > 2.0**-80) & (jnp.max(lim[1]) < 2.0**100)

    out[:, 0:EARLY] = early[...]
    net.run(EARLY, states - EARLY, lambda s: net.attention(s, False), fetch, out, 0)

    @pl.when(jnp.logical_not(within(lims) & within(net.lim)))
    def _():
        net.run(0, states, lambda s: net.attention(s, True), fetch, out, 0)


def rest(every, early, lims, ws, states):
    return pl.pallas_call(
        functools.partial(rest_kernel, states),
        out_shape=jax.ShapeDtypeStruct((2, states, 128), f32),
        in_specs=[ANY] + [V] * 8,
        out_specs=V,
        scratch_shapes=scratch(),
        compiler_params=pltpu.CompilerParams(vmem_limit_bytes=56 * 2**20),
    )(every, early, lims, *ws)


def solve_kernel(states, walks, *refs):
    parts, pot, energy, mean, mat, rows, ssem, rsem, wssem, wrsem = refs
    me, mw = lax.axis_index("state"), lax.axis_index("walk")
    barrier = pltpu.get_barrier_semaphore()
    for d in range(1, states):
        pl.semaphore_signal(barrier, inc=1, device_id=(lax.rem(me + d, states), mw), device_id_type=MESH)
    for d in range(1, walks):
        pl.semaphore_signal(barrier, inc=1, device_id=(me, lax.rem(mw + d, walks)), device_id_type=MESH)

    lane = lax.broadcasted_iota(jnp.int32, (states, 128), 1)
    row_at = lax.broadcasted_iota(jnp.int32, (states, 128), 0)
    offset = functools.reduce(lambda a, p: jnp.where(row_at == p, OFFSETS[p], a), range(states), row_at)
    config = jnp.bitwise_xor(offset, me)

    def spread(t):
        value = jnp.sum(parts[t], axis=1, keepdims=True)
        return jnp.sum(jnp.where(lane == config + (1 - t) * states, value, 0.0), axis=0, keepdims=True)

    lane1 = lane[0:1]
    amp = spread(0)
    ham = spread(1)
    eye = jnp.where(lane1 == me + states, 1.0, 0.0)
    psi = jnp.where(lane1 < states, 0.0, eye + 0.9 / states * jnp.tanh(amp))
    mat[pl.ds(me, 1), :] = ham + jnp.where(lane1 < 2 * states, psi, 0.0)
    pl.semaphore_wait(barrier, states - 1 + walks - 1)

    def send(d):
        return pltpu.make_async_remote_copy(
            src_ref=mat.at[pl.ds(me, 1)], dst_ref=mat.at[pl.ds(me, 1)], send_sem=ssem.at[d], recv_sem=rsem.at[d],
            device_id=(lax.rem(me + d, states), mw), device_id_type=MESH,
        )

    for d in range(1, states):
        send(d).start()
    for d in range(1, states):
        came = lax.rem(me + states - d, states)
        pltpu.make_async_remote_copy(
            src_ref=mat.at[pl.ds(me, 1)], dst_ref=mat.at[pl.ds(came, 1)], send_sem=ssem.at[d], recv_sem=rsem.at[d],
            device_id=(lax.rem(me + d, states), mw), device_id_type=MESH,
        ).wait_recv()
    m = mat[...]
    for k in range(states):
        pivot_row = m[k : k + 1, :]
        scaled = pivot_row / pivot_row[:, states + k : states + k + 1]
        column = m[:, states + k : states + k + 1]
        m = jnp.where(row_at == k, scaled, m - column * scaled)
    mine = jnp.sum(jnp.where(row_at == me, m, 0.0), axis=0, keepdims=True)
    mine = jnp.where(lane1 == me, mine + pot[...], mine)
    energy[...] = mine
    rows[pl.ds(mw, 1), :] = mine

    def send_row(d):
        return pltpu.make_async_remote_copy(
            src_ref=rows.at[pl.ds(mw, 1)], dst_ref=rows.at[pl.ds(mw, 1)], send_sem=wssem.at[d], recv_sem=wrsem.at[d],
            device_id=(me, lax.rem(mw + d, walks)), device_id_type=MESH,
        )

    for d in range(1, walks):
        send_row(d).start()
    for d in range(1, walks):
        came = lax.rem(mw + walks - d, walks)
        pltpu.make_async_remote_copy(
            src_ref=rows.at[pl.ds(mw, 1)], dst_ref=rows.at[pl.ds(came, 1)], send_sem=wssem.at[d], recv_sem=wrsem.at[d],
            device_id=(me, lax.rem(mw + d, walks)), device_id_type=MESH,
        ).wait_recv()
    mean[...] = jnp.sum(rows[...], axis=0, keepdims=True) * (1.0 / walks)
    for d in range(1, states):
        send(d).wait_send()
    for d in range(1, walks):
        send_row(d).wait_send()


def solve(parts, potential, states, walks):
    dma = pltpu.SemaphoreType.DMA
    return pl.pallas_call(
        functools.partial(solve_kernel, states, walks),
        out_shape=(jax.ShapeDtypeStruct((1, 128), f32), jax.ShapeDtypeStruct((1, 128), f32)),
        in_specs=[V, V],
        out_specs=(V, V),
        scratch_shapes=[
            pltpu.VMEM((states, 128), f32),
            pltpu.VMEM((walks, 128), f32),
            dma((states,)), dma((states,)), dma((walks,)), dma((walks,)),
        ],
        compiler_params=pltpu.CompilerParams(collective_id=0, has_side_effects=True),
    )(parts, potential)


def trim_kernel(energy, mean, energy_out, mean_out):
    n = energy_out.shape[1]
    energy_out[...] = energy[:, :n]
    mean_out[...] = mean[:, :n]


def trim(energy, mean, states):
    shape = jax.ShapeDtypeStruct((1, states), f32)
    return pl.pallas_call(trim_kernel, out_shape=(shape, shape), in_specs=[V, V], out_specs=(V, V))(energy, mean)


def local(features, key_blocks, block_counts, potential, w_qkv, w_out, w_up, w_down, gains, readouts):
    states, walks = lax.axis_size("state"), lax.axis_size("walk")
    ws = (w_qkv[0], w_out[0], w_up[0], w_down[0], gains.transpose(1, 0, 2), readouts[0])
    every, early, lims = gather(features[0, 0], key_blocks[0].transpose(2, 0, 1), block_counts[0], ws, states)
    parts = rest(every, early, lims, ws, states)
    energy, mean = trim(*solve(parts, potential, states, walks), states)
    return energy[:, :, None], mean


def solution(mesh):
    placed = (
        P("state", "walk", None, None),
        P("state", "walk", None, None),
        P("state", "walk", None),
        P("state", "walk"),
        P("state", None, None, None),
        P("state", None, None, None),
        P("state", None, None, None),
        P("state", None, None, None),
        P("state", None, None),
        P("state", None, None),
    )
    return jax.shard_map(
        local,
        mesh=mesh,
        in_specs=placed,
        out_specs=(P("state", None, "walk"), P("state", None)),
        check_vma=False,
    )
```
